32 devices in a mesh: groups: 2 (over y), dc: 4 (over z), tp: 2 (over x), sp: 2 (over core).
Axes of the slice: x: 2, y: 2, z: 4, core: 2. Of those that a mesh axis runs over, the one named last changes fastest.
Arguments:
- q_gen: bfloat16 [2048, 8192], P(('groups', 'dc', 'sp'), 'tp'), parts along dimension 0, may hold values from -32 to 32
- k_gen: bfloat16 [2048, 1024], P(('groups', 'dc', 'sp'), 'tp'), parts along dimension 0, may hold values from -8 to 8
- value_generator_rows: bfloat16 [2048, 1024], P(('groups', 'dc', 'sp'), 'tp'), parts along dimension 0, may hold values from -18 to 18
- w_reward: float32 [8192], P('tp'), may hold values from -0.2 to 0.2
- plan: int32 [3, 8], P(None, 'groups'), parts along dimension 1, may hold values from 0 to 512, as said below
- gen_order: int32 [16, 8], P(('groups', 'dc', 'sp')), parts along dimension 0, may hold values from 0 to 7, as said below
Outputs:
- scored: bfloat16 [2048, 8192], P(('groups', 'dc', 'sp'), 'tp'), parts along dimension 0
- reward: float32 [2048], P(('groups', 'dc', 'sp')), parts along dimension 0
The draws below stay inside these ranges and needn't reach their ends.
There are 2 independent parts, one for each index of `groups`. The reference program is written for one: setup_inputs(seed, part) draws one part's arguments, and reference() takes and returns one part's arrays. A program takes and returns all parts, laid end to end along the dimension named above; an argument that names none is the same for every part. Nothing has to cross between parts.
Inputs may be any that keep to these rules, and one draw needn't show every extreme that they name: `plan`: row 0 gives each dc index the first dc index of its rollout's subgroup, row 1 the subgroup's size, row 2 the rollout's length in tokens. Subgroups are aligned runs of 2 or 2 / 2 dc indices (2 or 1 here, 16 or 8 on the larger slice), and every draw has one subgroup of exactly 2 indices whose rollout has the full 2 * 256 tokens. A rollout on g indices has more than g * 128 and at most g * 256 tokens. `gen_order`: each row is a permutation of the 8 plan devices.
All inputs are finite; a program needn't handle non-finite values.
Results may differ from the reference program's by a relative error of at most 0.0048.
Values may be sent and summed in bfloat16 or wider, within the bound.
A program may use at most 64 MiB of HBM per device.

```python
import jax
import jax.numpy as jnp
from jax import lax

QUERY_HEADS = 64
KEY_VALUE_HEADS = 8
HEAD_WIDTH = 128
TOKENS_PER_SHARD = 128
RANKS = 8
SLOT = 256
PACKED_TOKENS = 1024
MAXG = 2
N_DC = 4


def shared_keys(key):
    bell_curve = jax.random.normal(jax.random.fold_in(key, 101), (PACKED_TOKENS, KEY_VALUE_HEADS * HEAD_WIDTH), jnp.float32)
    base_offset = bell_curve
    return base_offset


def query_draw(key):
    bell_curve = jax.random.normal(jax.random.fold_in(key, 1), (PACKED_TOKENS, QUERY_HEADS * HEAD_WIDTH), jnp.float32)
    base_offset = bell_curve
    return base_offset


def draw_k_gen(key, part):
    return shared_keys(key).astype(jnp.bfloat16)


def draw_q_gen(key, part):
    key = jax.random.fold_in(key, 3)
    return query_draw(key).astype(jnp.bfloat16)


def draw_plan(key, part):
    key = jax.random.fold_in(key, 11)
    index = jnp.arange(N_DC, dtype=jnp.int32)
    chosen = jax.random.randint(jax.random.fold_in(key, 1), (), 0, N_DC // MAXG)
    size = jnp.full((N_DC,), MAXG, jnp.int32)
    for level in range(min(MAXG.bit_length() - 1, 1)):
        flags = jax.random.randint(jax.random.fold_in(key, 20 + level), (N_DC,), 0, 2)
        flag = flags[index // MAXG]
        flag = jnp.where(index // MAXG == chosen, 0, flag)
        size = jnp.where(flag == 0, size, size // 2)
    first_entry = index - index % size
    spare = size * SLOT // 2
    raw = jax.random.randint(jax.random.fold_in(key, 2), (N_DC,), 0, 1 << 20)
    length = spare + 1 + raw[first_entry] % spare
    length = jnp.where(index // MAXG == chosen, MAXG * SLOT, length)
    return jnp.stack([first_entry, size, length]).astype(jnp.int32)


def draw_gen_order(key, part):
    key = jax.random.fold_in(key, 13)
    key_rows = jax.random.split(key, RANKS)
    return jax.vmap(lambda single: jax.random.permutation(single, RANKS))(key_rows).astype(jnp.int32)


def levels(stream_key, shape, cuts, low, top_value):
    level = 1.0
    for dim, parts in cuts:
        heights = jax.random.uniform(jax.random.fold_in(jax.random.fold_in(stream_key, 6), dim), (parts,), jnp.float32, low / len(cuts), top_value / len(cuts))
        level = level * jnp.repeat(jnp.exp(heights), shape[dim] // parts).reshape((-1,) + (1,) * (len(shape) - 1 - dim))
    return level


def scatter_about(key, dims, deviation, most, shards=(), kind=jnp.bfloat16):
    level = levels(key, dims, shards, -0.22, 0.18) if shards else 1.0
    entries = jax.random.normal(key, dims, jnp.float32) * deviation * level
    return jnp.minimum(jnp.maximum(entries, -most), most).astype(kind)


def setup_inputs(seed: int = 0, part: int = 0) -> dict:
    arg_keys = jax.random.split(jax.random.key(seed), 7)
    part_keys = jax.random.split(jax.random.fold_in(arg_keys[6], part), 7)
    return {
        "q_gen": draw_q_gen(jax.random.fold_in(jax.random.fold_in(arg_keys[6], part), 71), part),
        "k_gen": draw_k_gen(jax.random.fold_in(jax.random.fold_in(arg_keys[6], part), 71), part),
        "value_generator_rows": scatter_about(part_keys[2], (PACKED_TOKENS, KEY_VALUE_HEADS * HEAD_WIDTH), 3.0, 18.0, ((0, 8), (1, 2))),
        "w_reward": scatter_about(arg_keys[3], (QUERY_HEADS * HEAD_WIDTH,), 0.03, 0.2, ((0, 2),), jnp.float32),
        "plan": draw_plan(jax.random.fold_in(jax.random.fold_in(arg_keys[6], part), 71), part),
        "gen_order": draw_gen_order(jax.random.fold_in(jax.random.fold_in(arg_keys[6], part), 71), part),
    }


NEG = -1.0e30


def reference(q_gen, k_gen, value_generator_rows, w_reward, plan, gen_order):
    ranks = RANKS
    piece = TOKENS_PER_SHARD // ranks
    rollout_group = QUERY_HEADS // KEY_VALUE_HEADS
    window_span = MAXG * SLOT
    labels = jnp.arange(ranks, dtype=jnp.int32)
    offsets = jnp.arange(piece, dtype=jnp.int32)[None, None, :]
    inverse = jnp.sum(jnp.where(gen_order[:, :, None] == labels[None, None, :], labels[None, :, None], 0), axis=1).astype(jnp.int32)
    source = (labels[None, :, None] * TOKENS_PER_SHARD + jnp.transpose(inverse)[:, :, None] * piece + offsets).reshape(-1)
    query_layout = jnp.take(q_gen, source, axis=0)
    key_layout = jnp.take(k_gen, source, axis=0)
    value_layout = jnp.take(value_generator_rows, source, axis=0)
    rows_all = jnp.arange(PACKED_TOKENS, dtype=jnp.int32)
    dc_index = rows_all // SLOT
    start = plan[0][dc_index]
    position = rows_all - start * SLOT
    valid = position < plan[2][dc_index]

    def one_rank(rank):
        first_entry = (rank * TOKENS_PER_SHARD).astype(jnp.int32)
        base_offset = ((rank * TOKENS_PER_SHARD) // window_span * window_span).astype(jnp.int32)
        query_rows = lax.dynamic_slice_in_dim(query_layout, first_entry, TOKENS_PER_SHARD, 0).astype(jnp.float32).reshape(TOKENS_PER_SHARD, KEY_VALUE_HEADS, rollout_group, HEAD_WIDTH)
        key_rows = lax.dynamic_slice_in_dim(key_layout, base_offset, window_span, 0).astype(jnp.float32).reshape(window_span, KEY_VALUE_HEADS, HEAD_WIDTH)
        value_rows = lax.dynamic_slice_in_dim(value_layout, base_offset, window_span, 0).astype(jnp.float32).reshape(window_span, KEY_VALUE_HEADS, HEAD_WIDTH)
        q_start = lax.dynamic_slice_in_dim(start, first_entry, TOKENS_PER_SHARD, 0)
        q_pos = lax.dynamic_slice_in_dim(position, first_entry, TOKENS_PER_SHARD, 0)
        q_valid = lax.dynamic_slice_in_dim(valid, first_entry, TOKENS_PER_SHARD, 0)
        k_start = lax.dynamic_slice_in_dim(start, base_offset, window_span, 0)
        k_pos = lax.dynamic_slice_in_dim(position, base_offset, window_span, 0)
        allowed = (q_start[:, None] == k_start[None, :]) & (k_pos[None, :] <= q_pos[:, None])
        scores = jnp.einsum('rjge,nje->jgrn', query_rows, key_rows) * (HEAD_WIDTH ** -0.5)
        scores = jnp.where(allowed, scores, NEG)
        top = jnp.max(scores, axis=-1, keepdims=True)
        weight = jnp.where(allowed, jnp.exp(scores - top), 0.0)
        total = jnp.sum(weight, axis=-1)
        rounded = lax.optimization_barrier(weight.astype(jnp.bfloat16))
        mixed = jnp.einsum('jgrn,nje->rjge', rounded.astype(jnp.float32), value_rows)
        mixed = mixed / jnp.transpose(total, (2, 0, 1))[..., None]
        mixed = jnp.where(q_valid[:, None, None, None], mixed, 0.0)
        return mixed.reshape(TOKENS_PER_SHARD, QUERY_HEADS * HEAD_WIDTH).astype(jnp.bfloat16)

    hidden = lax.map(one_rank, labels).reshape(PACKED_TOKENS, QUERY_HEADS * HEAD_WIDTH)
    back = (gen_order[:, :, None] * TOKENS_PER_SHARD + labels[:, None, None] * piece + offsets).reshape(-1)
    scored = jnp.take(hidden, back, axis=0)
    reward = jnp.sum(scored.astype(jnp.float32) * w_reward[None, :], axis=1)
    return scored, reward
```

```python
import functools

import jax
import jax.numpy as jnp
from jax import lax
from jax.experimental import pallas as pl
from jax.experimental.pallas import tpu as pltpu
from jax.sharding import PartitionSpec as P

HEAD_WIDTH = 128


NEG = -1e30


def from_behind(block, axis, distance):
    devices = range(lax.axis_size(axis))
    route = [(i - distance, i) for i in devices if i - distance in devices]
    return lax.ppermute(block, axis, route)


def fold_block(state, key_rows, value_rows, query_rows, allowed, scale):
    top, total, mixed = state
    scores = (
        jnp.einsum("rjge,nje->jgrn", query_rows, key_rows, preferred_element_type=jnp.float32)
        * scale
    )
    if allowed is not None:
        scores = jnp.where(allowed, scores, NEG)
    newtop = jnp.maximum(top, jnp.max(scores, axis=-1))
    shrink = jnp.exp(top - newtop)
    weight = jnp.exp(scores - newtop[..., None])
    if allowed is not None:
        weight = jnp.where(allowed, weight, 0.0)
    total = total * shrink + jnp.sum(weight, axis=-1)
    update = jnp.einsum(
        "jgrn,nje->jgre",
        weight.astype(jnp.bfloat16),
        value_rows,
        preferred_element_type=jnp.float32,
    )
    return (newtop, total, mixed * shrink[..., None] + update)


def body(q_gen, k_gen, value_generator_rows, w_reward, plan, gen_order):
    ranks = lax.axis_size(("dc", "sp"))
    sp_size = lax.axis_size("sp")
    dc_size = ranks // sp_size
    rows = q_gen.shape[0]
    piece = rows // ranks
    width_q = q_gen.shape[1]
    width_kv = k_gen.shape[1]
    heads_kv = width_kv // HEAD_WIDTH
    rollout_group = width_q // HEAD_WIDTH // heads_kv
    scale = HEAD_WIDTH ** (-0.5)
    order_row = gen_order[0]
    labels = jnp.arange(ranks, dtype=jnp.int32)
    inverse = jnp.sum(jnp.where(order_row[:, None] == labels[None, :], labels[:, None], 0), axis=0)
    q_send = jnp.take(q_gen.reshape(ranks, piece, width_q), inverse, axis=0)
    k_send = jnp.take(k_gen.reshape(ranks, piece, width_kv), inverse, axis=0)
    v_send = jnp.take(value_generator_rows.reshape(ranks, piece, width_kv), inverse, axis=0)
    q_flat = q_send.reshape(rows, width_q)
    k_flat = k_send.reshape(rows, width_kv)
    v_flat = v_send.reshape(rows, width_kv)
    query_layout, key_layout, value_layout = (
        lax.all_to_all(q_flat, ("dc", "sp"), split_axis=0, concat_axis=0, tiled=True),
        lax.all_to_all(k_flat, ("dc", "sp"), split_axis=0, concat_axis=0, tiled=True),
        lax.all_to_all(v_flat, ("dc", "sp"), split_axis=0, concat_axis=0, tiled=True),
    )
    me = lax.axis_index(("dc", "sp"))
    my_dc = me // sp_size
    start = plan[0, my_dc]
    length = plan[2, my_dc]
    local = jnp.arange(rows, dtype=jnp.int32)
    position = (my_dc - start) * (rows * sp_size) + me % sp_size * rows + local
    valid = position < length
    query_rows = query_layout.reshape(rows, heads_kv, rollout_group, HEAD_WIDTH)
    state = (
        jnp.full((heads_kv, rollout_group, rows), NEG, jnp.float32),
        jnp.zeros((heads_kv, rollout_group, rows), jnp.float32),
        jnp.zeros((heads_kv, rollout_group, rows, HEAD_WIDTH), jnp.float32),
    )
    causal = local[None, :] <= local[:, None]
    state = fold_block(
        state,
        key_layout.reshape(rows, heads_kv, HEAD_WIDTH),
        value_layout.reshape(rows, heads_kv, HEAD_WIDTH),
        query_rows,
        causal,
        scale,
    )
    own = jnp.stack([key_layout, value_layout])
    reach = max(dc_size // 2, 1) * sp_size

    def advance(step, carry):
        folded, moving = carry
        moving = from_behind(moving, ("dc", "sp"), 1)
        source = me - step - 1
        use = (source >= 0) & (source // sp_size >= start)
        folded = lax.cond(
            use,
            lambda carried: fold_block(
                carried,
                moving[0].reshape(rows, heads_kv, HEAD_WIDTH),
                moving[1].reshape(rows, heads_kv, HEAD_WIDTH),
                query_rows,
                None,
                scale,
            ),
            lambda carried: carried,
            folded,
        )
        return (folded, moving)

    state, _ = lax.fori_loop(0, reach - 1, advance, (state, own))
    top, total, mixed = state
    hidden = mixed / total[..., None]
    hidden = jnp.transpose(hidden, (2, 0, 1, 3)).reshape(rows, width_q)
    hidden = jnp.where(valid[:, None], hidden, 0.0).astype(jnp.bfloat16)
    back = lax.all_to_all(hidden, ("dc", "sp"), split_axis=0, concat_axis=0, tiled=True)
    scored = jnp.take(back.reshape(ranks, piece, width_q), order_row, axis=0).reshape(rows, width_q)
    partial_reward = jnp.sum(scored.astype(jnp.float32) * w_reward[None, :], axis=1)
    reward = lax.psum(partial_reward, "tp")
    return (scored, reward)


MESH = pl.DeviceIdType.MESH
BIG = -1e30


def gather_attend(
    sizes, order_ref, plan_ref, q_ref, k_ref, v_ref, w_ref, out_ref, rew_ref,
    q_send, q_all, kv_send, kv_all, hid_send, hid_all, racc, rew_all,
    kv_ssem, kv_rsem, fwd_ssem, q_ssem, q_rsem, hid_ssem, hid_rsem, rew_ssem, rew_rsem,
):
    dcs, sps, tps, piece, rows, heads, group, jc, span, halves = sizes
    ranks, units, width = dcs * sps, jc * halves, group * HEAD_WIDTH
    dc, sp, tp = lax.axis_index("dc"), lax.axis_index("sp"), lax.axis_index("tp")
    me, other = dc * sps + sp, 1 - sp

    barrier = pltpu.get_barrier_semaphore()
    for rank in range(ranks):
        @pl.when(rank != me)
        def _():
            pl.semaphore_signal(
                barrier, inc=1, device_id={"dc": rank // sps, "sp": rank % sps}, device_id_type=MESH
            )
    for shift in range(1, tps):
        for core in range(sps):
            pl.semaphore_signal(
                barrier, inc=1, device_id={"tp": lax.rem(tp + shift, tps), "sp": core}, device_id_type=MESH
            )

    for d in range(ranks):
        seg = jnp.int32(0)
        for s in range(1, ranks):
            seg = jnp.where(order_ref[0, s] == d, s, seg)
        h, dl = d // span, d % span
        for jj in range(jc):
            u = jj * halves + h
            for core in range(sps):
                head = core * jc + jj
                cols = pl.ds(head * HEAD_WIDTH, HEAD_WIDTH)
                kv_send[core, u, 0, pl.ds(dl * piece, piece), :] = k_ref[seg, :, cols]
                kv_send[core, u, 1, pl.ds(dl * piece, piece), :] = v_ref[seg, :, cols]
            mine = pl.ds(pl.multiple_of((sp * jc + jj) * width, width), width)
            theirs = pl.ds(pl.multiple_of((other * jc + jj) * width, width), width)
            q_all[0, u, dl] = q_ref[seg, :, mine]
            q_send[u, dl] = q_ref[seg, :, theirs]

    pl.semaphore_wait(barrier, ranks - 1 + (tps - 1) * sps)

    steps = [sign * hop for hop in (1, 2) if hop < dcs for sign in (1, -1)]

    def kv_copy(u, i, core):
        return pltpu.make_async_remote_copy(
            src_ref=kv_send.at[core, u], dst_ref=kv_all.at[u, me],
            send_sem=kv_ssem.at[u, i * sps + core], recv_sem=kv_rsem.at[u, me],
            device_id={"dc": dc + steps[i], "sp": core}, device_id_type=MESH,
        )

    def kv_copy_sibling(u):
        return pltpu.make_async_remote_copy(
            src_ref=kv_send.at[other, u], dst_ref=kv_all.at[u, me],
            send_sem=kv_ssem.at[u, len(steps) * sps], recv_sem=kv_rsem.at[u, me],
            device_id={"sp": other}, device_id_type=MESH,
        )

    def kv_forward(u, core, source_dc, target_dc):
        source = source_dc * sps + core
        return pltpu.make_async_remote_copy(
            src_ref=kv_all.at[u, source], dst_ref=kv_all.at[u, source],
            send_sem=fwd_ssem.at[u, core], recv_sem=kv_rsem.at[u, source],
            device_id={"dc": target_dc}, device_id_type=MESH,
        )

    def kv_wait(u, source):
        pltpu.make_async_remote_copy(
            src_ref=kv_all.at[u, source], dst_ref=kv_all.at[u, source],
            send_sem=kv_ssem.at[u, 0], recv_sem=kv_rsem.at[u, source],
            device_id={"sp": other}, device_id_type=MESH,
        ).wait_recv()

    q_copy = pltpu.make_async_remote_copy(
        src_ref=q_send, dst_ref=q_all.at[1], send_sem=q_ssem, recv_sem=q_rsem,
        device_id={"sp": other}, device_id_type=MESH,
    )

    def send_unit(u, carry):
        for i, step in enumerate(steps):
            @pl.when((dc + step >= 0) & (dc + step < dcs))
            def _():
                for core in range(sps):
                    kv_copy(u, i, core).start()
        kv_copy_sibling(u).start()
        kv_all[u, me] = kv_send[sp, u]
        return carry

    lax.fori_loop(0, units, send_unit, 0)
    q_copy.start()

    tile = 2 * group * piece
    row = lax.broadcasted_iota(jnp.int32, (tile, 1), 0)
    rank_of_row = dc * sps + jnp.where(row < group * piece, sp, other)
    offset = rank_of_row * piece + lax.rem(row, piece)
    column = lax.broadcasted_iota(jnp.int32, (tile, rows), 1)
    causal = jnp.where(column <= offset, 0.0, BIG)
    factor = HEAD_WIDTH ** (-0.5) * 1.4426950408889634

    def hid_copy(u):
        return pltpu.make_async_remote_copy(
            src_ref=hid_send.at[u], dst_ref=hid_all.at[sp, u],
            send_sem=hid_ssem.at[u], recv_sem=hid_rsem.at[u],
            device_id={"sp": other}, device_id_type=MESH,
        )

    q_copy.wait_recv()

    def attend(u, carry):
        jj, h = u // halves, lax.rem(u, halves)
        if dcs == 4:
            for relay, far, end in ((1, 3, 0), (2, 0, 3)):
                @pl.when(dc == relay)
                def _():
                    for core in range(sps):
                        kv_wait(u, far * sps + core)
                        kv_forward(u, core, far, end).start()
        for source in range(ranks):
            sdc = source // sps
            waits = source != me
            if dcs == 4 and sdc in (0, 3):
                waits = waits & (dc != (2 if sdc == 0 else 1))

            @pl.when(waits)
            def _():
                kv_wait(u, source)

        def plan_order(which):
            return jnp.concatenate(
                [
                    kv_all[u, source, which, pl.ds(dl * piece, piece), :]
                    for dl in range(span)
                    for source in range(ranks)
                ],
                axis=0,
            )

        keys, values = plan_order(0), plan_order(1)
        for dl in range(span):
            d = h * span + dl
            slot = d // sps
            n = (dl + 1) * rows
            query = jnp.concatenate(
                [
                    q_all[t, u, dl, :, pl.ds(g * HEAD_WIDTH, HEAD_WIDTH)]
                    for t in range(2)
                    for g in range(group)
                ],
                axis=0,
            )
            scores = lax.dot_general(
                query, keys[:n], (((1,), (1,)), ((), ())), preferred_element_type=jnp.float32
            )
            start = plan_ref[0, slot]
            blocks = []
            for d2 in range(dl + 1):
                block = scores[:, d2 * rows:(d2 + 1) * rows]
                if d2 == dl:
                    block = block + causal
                elif d2 // sps != dl // sps:
                    block = block + jnp.where(plan_ref[0, h * (span // sps) + d2 // sps] == start, 0.0, BIG)
                blocks.append(block)
            peak = blocks[0]
            for block in blocks[1:]:
                peak = jnp.maximum(peak, block)
            top = jnp.max(peak, axis=1, keepdims=True)
            weights = [jnp.exp2((block - top) * factor) for block in blocks]
            total = weights[0]
            for weight in weights[1:]:
                total = total + weight
            total = jnp.sum(total, axis=1, keepdims=True)
            weight16 = jnp.concatenate([weight.astype(jnp.bfloat16) for weight in weights], axis=1)
            mixed = jnp.dot(weight16, values[:n], preferred_element_type=jnp.float32)
            base = (slot - start) * (rows * sps) + lax.rem(d, sps) * rows
            share = jnp.where(offset + base < plan_ref[2, slot], 1.0 / total, 0.0)
            hidden = (mixed * share).astype(jnp.bfloat16)
            for t in range(2):
                reward = jnp.zeros((piece, HEAD_WIDTH), jnp.float32)
                for g in range(group):
                    part = hidden[(t * group + g) * piece:(t * group + g + 1) * piece]
                    cols = pl.ds(g * HEAD_WIDTH, HEAD_WIDTH)
                    if t == 0:
                        hid_all[sp, u, dl, :, cols] = part
                    else:
                        hid_send[u, dl, :, cols] = part
                    w = w_ref[sp * jc + jj, pl.ds(g, 1), :]
                    reward = reward + part.astype(jnp.float32) * w
                racc[u, t, pl.ds(dl * piece, piece), :] = reward
        hid_copy(u).start()
        return carry

    lax.fori_loop(0, units, attend, 0)

    sums = []
    for t in range(2):
        cells = []
        for h in range(halves):
            cell = racc[h, t]
            for jj in range(1, jc):
                cell = cell + racc[jj * halves + h, t]
            cells.append(cell)
        line = jnp.sum(jnp.concatenate(cells, axis=0).T, axis=0, keepdims=True)
        sums.append(jnp.broadcast_to(line, (8, rows)))
    slot_me = tp * sps + sp
    rew_all[tps * sps] = sums[1]
    rew_all[slot_me] = sums[0]

    def rew_copy(shift, same):
        peer = lax.rem(tp + shift, tps)
        return pltpu.make_async_remote_copy(
            src_ref=rew_all.at[slot_me if same else tps * sps], dst_ref=rew_all.at[slot_me],
            send_sem=rew_ssem.at[2 * shift + (0 if same else 1)], recv_sem=rew_rsem.at[slot_me],
            device_id={"tp": peer, "sp": sp if same else other}, device_id_type=MESH,
        )

    pairs = [(shift, same) for shift in range(tps) for same in (True, False) if (shift, same) != (0, True)]
    for shift, same in pairs:
        rew_copy(shift, same).start()

    for u in range(units):
        hid_copy(u).wait_recv()
    for s in range(ranks):
        d = order_ref[0, s]
        h, dl = d // span, lax.rem(d, span)
        for core in range(sps):
            for jj in range(jc):
                out_ref[s, :, pl.ds((core * jc + jj) * width, width)] = hid_all[core, jj * halves + h, dl]

    for source in range(tps * sps):
        @pl.when(source != slot_me)
        def _():
            pltpu.make_async_remote_copy(
                src_ref=rew_all.at[source], dst_ref=rew_all.at[source],
                send_sem=rew_ssem.at[0], recv_sem=rew_rsem.at[source],
                device_id={"sp": other}, device_id_type=MESH,
            ).wait_recv()
    reward = rew_all[0]
    for source in range(1, tps * sps):
        reward = reward + rew_all[source]
    rew_ref[...] = reward

    for shift, same in pairs:
        rew_copy(shift, same).wait_send()
    q_copy.wait_send()

    def drain(u, carry):
        hid_copy(u).wait_send()
        kv_copy_sibling(u).wait_send()
        for i, step in enumerate(steps):
            @pl.when((dc + step >= 0) & (dc + step < dcs))
            def _():
                for core in range(sps):
                    kv_copy(u, i, core).wait_send()
        if dcs == 4:
            for relay, far, end in ((1, 3, 0), (2, 0, 3)):
                @pl.when(dc == relay)
                def _():
                    for core in range(sps):
                        kv_forward(u, core, far, end).wait_send()
        return carry

    lax.fori_loop(0, units, drain, 0)


def gather_body(q_gen, k_gen, value_generator_rows, w_reward, plan, gen_order):
    dcs, sps, tps = lax.axis_size("dc"), lax.axis_size("sp"), lax.axis_size("tp")
    ranks = dcs * sps
    rows, width_q = q_gen.shape
    width_kv = k_gen.shape[1]
    piece = rows // ranks
    heads = width_kv // HEAD_WIDTH
    group = width_q // width_kv
    jc = heads // sps
    span = max(dcs // 2, 1) * sps
    halves = ranks // span
    units, width = jc * halves, group * HEAD_WIDTH
    sizes = (dcs, sps, tps, piece, rows, heads, group, jc, span, halves)
    bf16, f32 = jnp.bfloat16, jnp.float32
    vmem, smem = pl.BlockSpec(memory_space=pltpu.VMEM), pl.BlockSpec(memory_space=pltpu.SMEM)
    dma = pltpu.SemaphoreType.DMA
    scored, reward = pl.pallas_call(
        functools.partial(gather_attend, sizes),
        out_shape=(
            jax.ShapeDtypeStruct((ranks, piece, width_q), bf16),
            jax.ShapeDtypeStruct((8, rows), f32),
        ),
        in_specs=[smem, smem, vmem, vmem, vmem, vmem],
        out_specs=(vmem, vmem),
        scratch_shapes=[
            pltpu.VMEM((units, span, piece, width), bf16),
            pltpu.VMEM((2, units, span, piece, width), bf16),
            pltpu.VMEM((sps, units, 2, span * piece, HEAD_WIDTH), bf16),
            pltpu.VMEM((units, ranks, 2, span * piece, HEAD_WIDTH), bf16),
            pltpu.VMEM((units, span, piece, width), bf16),
            pltpu.VMEM((sps, units, span, piece, width), bf16),
            pltpu.VMEM((units, 2, span * piece, HEAD_WIDTH), f32),
            pltpu.VMEM((tps * sps + 1, 8, rows), f32),
            dma((units, 4 * sps + 1)),
            dma((units, ranks)),
            dma((units, sps)),
            dma,
            dma,
            dma((units,)),
            dma((units,)),
            dma((2 * tps,)),
            dma((tps * sps,)),
        ],
        compiler_params=pltpu.CompilerParams(
            collective_id=0, has_side_effects=True, vmem_limit_bytes=32 * 1024 * 1024
        ),
    )(
        gen_order,
        plan,
        q_gen.reshape(ranks, piece, width_q),
        k_gen.reshape(ranks, piece, width_kv),
        value_generator_rows.reshape(ranks, piece, width_kv),
        w_reward.reshape(heads, group, HEAD_WIDTH),
    )
    labels = jnp.arange(ranks, dtype=jnp.int32)
    pick = gen_order[0][:, None, None] == labels[None, :, None]
    reward = jnp.sum(jnp.where(pick, reward[0].reshape(1, ranks, piece), 0.0), axis=1).reshape(rows)
    return (scored.reshape(rows, width_q), reward)


def solution(mesh):
    in_specs = (
        P(("groups", "dc", "sp"), "tp"),
        P(("groups", "dc", "sp"), "tp"),
        P(("groups", "dc", "sp"), "tp"),
        P("tp"),
        P(None, "groups"),
        P(("groups", "dc", "sp"), None),
    )
    out_specs = (P(("groups", "dc", "sp"), "tp"), P(("groups", "dc", "sp")))

    def whole(q_gen, k_gen, value_generator_rows, w_reward, plan, gen_order):
        rows = q_gen.shape[0] // (mesh.shape["groups"] * mesh.shape["dc"] * mesh.shape["sp"])
        heads = k_gen.shape[1] // HEAD_WIDTH // mesh.shape["tp"]
        fits = (
            mesh.shape["dc"] in (2, 4)
            and mesh.shape["sp"] == 2
            and heads % 2 == 0
            and rows == HEAD_WIDTH
            and rows % (16 * mesh.shape["dc"] * mesh.shape["sp"]) == 0
        )
        inner = gather_body if fits else body
        return jax.shard_map(inner, mesh=mesh, in_specs=in_specs, out_specs=out_specs, check_vma=False)(
            q_gen, k_gen, value_generator_rows, w_reward, plan, gen_order
        )

    return whole
```

```python
import functools

import jax
import jax.numpy as jnp
from jax import lax
from jax.experimental import pallas as pl
from jax.experimental.pallas import tpu as pltpu
from jax.sharding import PartitionSpec as P

HEAD_WIDTH = 128


NEG = -1e30


def from_behind(block, axis, distance):
    devices = range(lax.axis_size(axis))
    route = [(i - distance, i) for i in devices if i - distance in devices]
    return lax.ppermute(block, axis, route)


def fold_block(state, key_rows, value_rows, query_rows, allowed, scale):
    top, total, mixed = state
    scores = (
        jnp.einsum("rjge,nje->jgrn", query_rows, key_rows, preferred_element_type=jnp.float32)
        * scale
    )
    if allowed is not None:
        scores = jnp.where(allowed, scores, NEG)
    newtop = jnp.maximum(top, jnp.max(scores, axis=-1))
    shrink = jnp.exp(top - newtop)
    weight = jnp.exp(scores - newtop[..., None])
    if allowed is not None:
        weight = jnp.where(allowed, weight, 0.0)
    total = total * shrink + jnp.sum(weight, axis=-1)
    update = jnp.einsum(
        "jgrn,nje->jgre",
        weight.astype(jnp.bfloat16),
        value_rows,
        preferred_element_type=jnp.float32,
    )
    return (newtop, total, mixed * shrink[..., None] + update)


def body(q_gen, k_gen, value_generator_rows, w_reward, plan, gen_order):
    ranks = lax.axis_size(("dc", "sp"))
    sp_size = lax.axis_size("sp")
    dc_size = ranks // sp_size
    rows = q_gen.shape[0]
    piece = rows // ranks
    width_q = q_gen.shape[1]
    width_kv = k_gen.shape[1]
    heads_kv = width_kv // HEAD_WIDTH
    rollout_group = width_q // HEAD_WIDTH // heads_kv
    scale = HEAD_WIDTH ** (-0.5)
    order_row = gen_order[0]
    labels = jnp.arange(ranks, dtype=jnp.int32)
    inverse = jnp.sum(jnp.where(order_row[:, None] == labels[None, :], labels[:, None], 0), axis=0)
    q_send = jnp.take(q_gen.reshape(ranks, piece, width_q), inverse, axis=0)
    k_send = jnp.take(k_gen.reshape(ranks, piece, width_kv), inverse, axis=0)
    v_send = jnp.take(value_generator_rows.reshape(ranks, piece, width_kv), inverse, axis=0)
    q_flat = q_send.reshape(rows, width_q)
    k_flat = k_send.reshape(rows, width_kv)
    v_flat = v_send.reshape(rows, width_kv)
    query_layout, key_layout, value_layout = (
        lax.all_to_all(q_flat, ("dc", "sp"), split_axis=0, concat_axis=0, tiled=True),
        lax.all_to_all(k_flat, ("dc", "sp"), split_axis=0, concat_axis=0, tiled=True),
        lax.all_to_all(v_flat, ("dc", "sp"), split_axis=0, concat_axis=0, tiled=True),
    )
    me = lax.axis_index(("dc", "sp"))
    my_dc = me // sp_size
    start = plan[0, my_dc]
    length = plan[2, my_dc]
    local = jnp.arange(rows, dtype=jnp.int32)
    position = (my_dc - start) * (rows * sp_size) + me % sp_size * rows + local
    valid = position < length
    query_rows = query_layout.reshape(rows, heads_kv, rollout_group, HEAD_WIDTH)
    state = (
        jnp.full((heads_kv, rollout_group, rows), NEG, jnp.float32),
        jnp.zeros((heads_kv, rollout_group, rows), jnp.float32),
        jnp.zeros((heads_kv, rollout_group, rows, HEAD_WIDTH), jnp.float32),
    )
    causal = local[None, :] <= local[:, None]
    state = fold_block(
        state,
        key_layout.reshape(rows, heads_kv, HEAD_WIDTH),
        value_layout.reshape(rows, heads_kv, HEAD_WIDTH),
        query_rows,
        causal,
        scale,
    )
    own = jnp.stack([key_layout, value_layout])
    reach = max(dc_size // 2, 1) * sp_size

    def advance(step, carry):
        folded, moving = carry
        moving = from_behind(moving, ("dc", "sp"), 1)
        source = me - step - 1
        use = (source >= 0) & (source // sp_size >= start)
        folded = lax.cond(
            use,
            lambda carried: fold_block(
                carried,
                moving[0].reshape(rows, heads_kv, HEAD_WIDTH),
                moving[1].reshape(rows, heads_kv, HEAD_WIDTH),
                query_rows,
                None,
                scale,
            ),
            lambda carried: carried,
            folded,
        )
        return (folded, moving)

    state, _ = lax.fori_loop(0, reach - 1, advance, (state, own))
    top, total, mixed = state
    hidden = mixed / total[..., None]
    hidden = jnp.transpose(hidden, (2, 0, 1, 3)).reshape(rows, width_q)
    hidden = jnp.where(valid[:, None], hidden, 0.0).astype(jnp.bfloat16)
    back = lax.all_to_all(hidden, ("dc", "sp"), split_axis=0, concat_axis=0, tiled=True)
    scored = jnp.take(back.reshape(ranks, piece, width_q), order_row, axis=0).reshape(rows, width_q)
    partial_reward = jnp.sum(scored.astype(jnp.float32) * w_reward[None, :], axis=1)
    reward = lax.psum(partial_reward, "tp")
    return (scored, reward)


MESH = pl.DeviceIdType.MESH
BIG = -1e30


def gather_attend(
    sizes, order_hbm, plan_hbm, q_hbm, k_hbm, v_hbm, w_hbm, out_ref, rew_ref, order_out,
    order_ref, plan_ref, q_ref, k_ref, v_ref, w_ref, q_send, q_all, kv_send, kv_all, hid_send, racc, rew_all,
    kv_ssem, kv_rsem, fwd_ssem, q_ssem, q_rsem, hid_ssem, hid_rsem, rew_ssem, rew_rsem, in_sem,
):
    dcs, sps, tps, piece, rows, heads, group, jc, span, halves = sizes
    ranks, units, width = dcs * sps, jc * halves, group * HEAD_WIDTH
    dc, sp, tp = lax.axis_index("dc"), lax.axis_index("sp"), lax.axis_index("tp")
    me, other = dc * sps + sp, 1 - sp

    arguments = ((order_hbm, order_ref), (k_hbm, k_ref), (v_hbm, v_ref), (q_hbm, q_ref), (plan_hbm, plan_ref), (w_hbm, w_ref))
    loads = [pltpu.make_async_copy(a, b, in_sem.at[i]) for i, (a, b) in enumerate(arguments)]
    for load in loads:
        load.start()

    barrier = pltpu.get_barrier_semaphore()
    for rank in range(ranks):
        @pl.when(rank != me)
        def _():
            pl.semaphore_signal(
                barrier, inc=1, device_id={"dc": rank // sps, "sp": rank % sps}, device_id_type=MESH
            )
    for shift in range(1, tps):
        for core in range(sps):
            pl.semaphore_signal(
                barrier, inc=1, device_id={"tp": lax.rem(tp + shift, tps), "sp": core}, device_id_type=MESH
            )

    for load in loads[:3]:
        load.wait()
    segments = []
    for d in range(ranks):
        seg = jnp.int32(0)
        for s in range(1, ranks):
            seg = jnp.where(order_ref[0, s] == d, s, seg)
        segments.append(seg)
    for d in range(ranks):
        h, dl = d // span, d % span
        for jj in range(jc):
            u = jj * halves + h
            for core in range(sps):
                cols = pl.ds((core * jc + jj) * HEAD_WIDTH, HEAD_WIDTH)
                kv_send[core, u, 0, pl.ds(dl * piece, piece), :] = k_ref[segments[d], :, cols]
                kv_send[core, u, 1, pl.ds(dl * piece, piece), :] = v_ref[segments[d], :, cols]

    pl.semaphore_wait(barrier, ranks - 1 + (tps - 1) * sps)

    steps = [sign * hop for hop in (1, 2) if hop < dcs for sign in (1, -1)]

    def kv_copy(u, i, core):
        return pltpu.make_async_remote_copy(
            src_ref=kv_send.at[core, u], dst_ref=kv_all.at[u, me],
            send_sem=kv_ssem.at[u, i * sps + core], recv_sem=kv_rsem.at[u, me],
            device_id={"dc": dc + steps[i], "sp": core}, device_id_type=MESH,
        )

    def kv_copy_sibling(u):
        return pltpu.make_async_remote_copy(
            src_ref=kv_send.at[other, u], dst_ref=kv_all.at[u, me],
            send_sem=kv_ssem.at[u, len(steps) * sps], recv_sem=kv_rsem.at[u, me],
            device_id={"sp": other}, device_id_type=MESH,
        )

    def kv_forward(u, core, source_dc, target_dc):
        source = source_dc * sps + core
        return pltpu.make_async_remote_copy(
            src_ref=kv_all.at[u, source], dst_ref=kv_all.at[u, source],
            send_sem=fwd_ssem.at[u, core], recv_sem=kv_rsem.at[u, source],
            device_id={"dc": target_dc}, device_id_type=MESH,
        )

    def kv_wait(u, source):
        pltpu.make_async_remote_copy(
            src_ref=kv_all.at[u, source], dst_ref=kv_all.at[u, source],
            send_sem=kv_ssem.at[u, 0], recv_sem=kv_rsem.at[u, source],
            device_id={"sp": other}, device_id_type=MESH,
        ).wait_recv()

    q_copy = pltpu.make_async_remote_copy(
        src_ref=q_send, dst_ref=q_all.at[1], send_sem=q_ssem, recv_sem=q_rsem,
        device_id={"sp": other}, device_id_type=MESH,
    )

    def send_unit(u, carry):
        for i, step in enumerate(steps):
            @pl.when((dc + step >= 0) & (dc + step < dcs))
            def _():
                for core in range(sps):
                    kv_copy(u, i, core).start()
        kv_copy_sibling(u).start()
        kv_all[u, me] = kv_send[sp, u]
        return carry

    lax.fori_loop(0, units, send_unit, 0)
    loads[3].wait()
    for d in range(ranks):
        h, dl = d // span, d % span
        for jj in range(jc):
            u = jj * halves + h
            mine = pl.ds(pl.multiple_of((sp * jc + jj) * width, width), width)
            theirs = pl.ds(pl.multiple_of((other * jc + jj) * width, width), width)
            q_send[u, dl] = q_ref[segments[d], :, theirs]
            q_all[0, u, dl] = q_ref[segments[d], :, mine]
    q_copy.start()
    for load in loads[4:]:
        load.wait()

    tile = 2 * group * piece
    row = lax.broadcasted_iota(jnp.int32, (tile, 1), 0)
    rank_of_row = dc * sps + jnp.where(row < group * piece, sp, other)
    offset = rank_of_row * piece + lax.rem(row, piece)
    column = lax.broadcasted_iota(jnp.int32, (tile, rows), 1)
    causal = jnp.where(column <= offset, 0.0, BIG)
    factor = HEAD_WIDTH ** (-0.5) * 1.4426950408889634

    def hid_place(u):
        head = sp * jc + u // halves
        return out_ref.at[
            pl.ds(lax.rem(u, halves) * span, span), :, pl.ds(pl.multiple_of(head * width, width), width)
        ]

    def hid_copy(u):
        return pltpu.make_async_remote_copy(
            src_ref=hid_send.at[u], dst_ref=hid_place(u),
            send_sem=hid_ssem.at[u], recv_sem=hid_rsem.at[u],
            device_id={"sp": other}, device_id_type=MESH,
        )

    q_copy.wait_recv()

    def attend(u, carry):
        jj, h = u // halves, lax.rem(u, halves)
        head = sp * jc + jj
        if dcs == 4:
            for relay, far, end in ((1, 3, 0), (2, 0, 3)):
                @pl.when(dc == relay)
                def _():
                    for core in range(sps):
                        kv_wait(u, far * sps + core)
                        kv_forward(u, core, far, end).start()
        for source in range(ranks):
            sdc = source // sps
            waits = source != me
            if dcs == 4 and sdc in (0, 3):
                waits = waits & (dc != (2 if sdc == 0 else 1))

            @pl.when(waits)
            def _():
                kv_wait(u, source)

        def plan_order(which):
            return jnp.concatenate(
                [
                    kv_all[u, source, which, pl.ds(dl * piece, piece), :]
                    for dl in range(span)
                    for source in range(ranks)
                ],
                axis=0,
            )

        keys, values = plan_order(0), plan_order(1)
        for dl in range(span):
            d = h * span + dl
            slot = d // sps
            n = (dl + 1) * rows
            query = jnp.concatenate(
                [
                    q_all[t, u, dl, :, pl.ds(g * HEAD_WIDTH, HEAD_WIDTH)]
                    for t in range(2)
                    for g in range(group)
                ],
                axis=0,
            )
            scores = lax.dot_general(
                query, keys[:n], (((1,), (1,)), ((), ())), preferred_element_type=jnp.float32
            )
            start = plan_ref[0, slot]
            blocks = []
            for d2 in range(dl + 1):
                block = scores[:, d2 * rows:(d2 + 1) * rows]
                if d2 == dl:
                    block = block + causal
                elif d2 // sps != dl // sps:
                    block = block + jnp.where(plan_ref[0, h * (span // sps) + d2 // sps] == start, 0.0, BIG)
                blocks.append(block)
            peak = blocks[0]
            for block in blocks[1:]:
                peak = jnp.maximum(peak, block)
            top = jnp.max(peak, axis=1, keepdims=True)
            weights = [jnp.exp2((block - top) * factor) for block in blocks]
            total = weights[0]
            for weight in weights[1:]:
                total = total + weight
            total = jnp.sum(total, axis=1, keepdims=True)
            weight16 = jnp.concatenate([weight.astype(jnp.bfloat16) for weight in weights], axis=1)
            mixed = jnp.dot(weight16, values[:n], preferred_element_type=jnp.float32)
            base = (slot - start) * (rows * sps) + lax.rem(d, sps) * rows
            share = jnp.where(offset + base < plan_ref[2, slot], 1.0 / total, 0.0)
            hidden = (mixed * share).astype(jnp.bfloat16)
            for t in range(2):
                reward = jnp.zeros((piece, HEAD_WIDTH), jnp.float32)
                for g in range(group):
                    part = hidden[(t * group + g) * piece:(t * group + g + 1) * piece]
                    cols = pl.ds(g * HEAD_WIDTH, HEAD_WIDTH)
                    if t == 0:
                        out_ref[d, :, pl.ds(pl.multiple_of(head * width, width) + g * HEAD_WIDTH, HEAD_WIDTH)] = part
                    else:
                        hid_send[u, dl, :, cols] = part
                    w = w_ref[sp * jc + jj, pl.ds(g, 1), :]
                    reward = reward + part.astype(jnp.float32) * w
                racc[u, t, pl.ds(dl * piece, piece), :] = reward
        hid_copy(u).start()
        return carry

    lax.fori_loop(0, units, attend, 0)

    sums = []
    for t in range(2):
        cells = []
        for h in range(halves):
            cell = racc[h, t]
            for jj in range(1, jc):
                cell = cell + racc[jj * halves + h, t]
            cells.append(cell)
        line = jnp.sum(jnp.concatenate(cells, axis=0).T, axis=0, keepdims=True)
        sums.append(jnp.broadcast_to(line, (8, rows)))
    slot_me = tp * sps + sp
    rew_all[tps * sps] = sums[1]
    rew_all[slot_me] = sums[0]

    def rew_copy(shift, same):
        peer = lax.rem(tp + shift, tps)
        return pltpu.make_async_remote_copy(
            src_ref=rew_all.at[slot_me if same else tps * sps], dst_ref=rew_all.at[slot_me],
            send_sem=rew_ssem.at[2 * shift + (0 if same else 1)], recv_sem=rew_rsem.at[slot_me],
            device_id={"tp": peer, "sp": sp if same else other}, device_id_type=MESH,
        )

    pairs = [(shift, same) for shift in range(tps) for same in (True, False) if (shift, same) != (0, True)]
    for shift, same in pairs:
        rew_copy(shift, same).start()

    for source in range(tps * sps):
        @pl.when(source != slot_me)
        def _():
            pltpu.make_async_remote_copy(
                src_ref=rew_all.at[source], dst_ref=rew_all.at[source],
                send_sem=rew_ssem.at[0], recv_sem=rew_rsem.at[source],
                device_id={"sp": other}, device_id_type=MESH,
            ).wait_recv()
    reward = rew_all[0]
    for source in range(1, tps * sps):
        reward = reward + rew_all[source]
    rew_ref[...] = reward
    for s in range(ranks):
        order_out[0, s] = order_ref[0, s]

    for shift, same in pairs:
        rew_copy(shift, same).wait_send()
    q_copy.wait_send()

    def drain(u, carry):
        hid_copy(u).wait()
        kv_copy_sibling(u).wait_send()
        for i, step in enumerate(steps):
            @pl.when((dc + step >= 0) & (dc + step < dcs))
            def _():
                for core in range(sps):
                    kv_copy(u, i, core).wait_send()
        if dcs == 4:
            for relay, far, end in ((1, 3, 0), (2, 0, 3)):
                @pl.when(dc == relay)
                def _():
                    for core in range(sps):
                        kv_forward(u, core, far, end).wait_send()
        return carry

    lax.fori_loop(0, units, drain, 0)


def to_generator_order(ranks, piece, order_ref, hidden, reward_ref, out, out_reward, line, sems):
    copies = [
        pltpu.make_async_copy(hidden.at[order_ref[0, s]], out.at[pl.ds(s * piece, piece)], sems.at[s])
        for s in range(ranks)
    ]
    for copy in copies:
        copy.start()
    reward = reward_ref[...]
    segment = lax.broadcasted_iota(jnp.int32, reward.shape, 1) // piece
    moved = reward
    for s in range(ranks):
        shift = lax.rem(s - order_ref[0, s] + ranks, ranks) * piece
        moved = jnp.where(segment == s, pltpu.roll(reward, shift, 1), moved)
    line[...] = moved[:1]
    last = pltpu.make_async_copy(line, out_reward, sems.at[ranks])
    last.start()
    for copy in copies + [last]:
        copy.wait()


def gather_body(q_gen, k_gen, value_generator_rows, w_reward, plan, gen_order):
    dcs, sps, tps = lax.axis_size("dc"), lax.axis_size("sp"), lax.axis_size("tp")
    ranks = dcs * sps
    rows, width_q = q_gen.shape
    width_kv = k_gen.shape[1]
    piece = rows // ranks
    heads = width_kv // HEAD_WIDTH
    group = width_q // width_kv
    jc = heads // sps
    span = max(dcs // 2, 1) * sps
    halves = ranks // span
    units, width = jc * halves, group * HEAD_WIDTH
    sizes = (dcs, sps, tps, piece, rows, heads, group, jc, span, halves)
    bf16, f32 = jnp.bfloat16, jnp.float32
    vmem, hbm = pl.BlockSpec(memory_space=pltpu.VMEM), pl.BlockSpec(memory_space=pltpu.HBM)
    smem = pl.BlockSpec(memory_space=pltpu.SMEM)
    dma = pltpu.SemaphoreType.DMA
    hidden, reward, order = pl.pallas_call(
        functools.partial(gather_attend, sizes),
        out_shape=(
            pltpu.VMEM((ranks, piece, width_q), bf16),
            pltpu.VMEM((8, rows), f32),
            pltpu.SMEM(gen_order.shape, jnp.int32),
        ),
        in_specs=[hbm] * 6,
        out_specs=(vmem, vmem, smem),
        scratch_shapes=[
            pltpu.SMEM(gen_order.shape, jnp.int32),
            pltpu.SMEM(plan.shape, jnp.int32),
            pltpu.VMEM((ranks, piece, width_q), bf16),
            pltpu.VMEM((ranks, piece, width_kv), bf16),
            pltpu.VMEM((ranks, piece, width_kv), bf16),
            pltpu.VMEM((heads, group, HEAD_WIDTH), f32),
            pltpu.VMEM((units, span, piece, width), bf16),
            pltpu.VMEM((2, units, span, piece, width), bf16),
            pltpu.VMEM((sps, units, 2, span * piece, HEAD_WIDTH), bf16),
            pltpu.VMEM((units, ranks, 2, span * piece, HEAD_WIDTH), bf16),
            pltpu.VMEM((units, span, piece, width), bf16),
            pltpu.VMEM((units, 2, span * piece, HEAD_WIDTH), f32),
            pltpu.VMEM((tps * sps + 1, 8, rows), f32),
            dma((units, 4 * sps + 1)),
            dma((units, ranks)),
            dma((units, sps)),
            dma,
            dma,
            dma((units,)),
            dma((units,)),
            dma((2 * tps,)),
            dma((tps * sps,)),
            dma((6,)),
        ],
        compiler_params=pltpu.CompilerParams(
            collective_id=0, has_side_effects=True, vmem_limit_bytes=32 * 1024 * 1024
        ),
    )(*[
        pltpu.with_memory_space_constraint(operand, pltpu.HBM)
        for operand in (
            gen_order,
            plan,
            q_gen.reshape(ranks, piece, width_q),
            k_gen.reshape(ranks, piece, width_kv),
            value_generator_rows.reshape(ranks, piece, width_kv),
            w_reward.reshape(heads, group, HEAD_WIDTH),
        )
    ])
    scored, reward = pl.pallas_call(
        functools.partial(to_generator_order, ranks, piece),
        out_shape=(pltpu.HBM((rows, width_q), bf16), pltpu.HBM((1, rows), f32)),
        in_specs=[smem, vmem, vmem],
        out_specs=(hbm, hbm),
        scratch_shapes=[pltpu.VMEM((1, rows), f32), dma((ranks + 1,))],
    )(order, pltpu.with_memory_space_constraint(hidden, pltpu.VMEM), pltpu.with_memory_space_constraint(reward, pltpu.VMEM))
    return (scored, reward.reshape(rows))


def solution(mesh):
    in_specs = (
        P(("groups", "dc", "sp"), "tp"),
        P(("groups", "dc", "sp"), "tp"),
        P(("groups", "dc", "sp"), "tp"),
        P("tp"),
        P(None, "groups"),
        P(("groups", "dc", "sp"), None),
    )
    out_specs = (P(("groups", "dc", "sp"), "tp"), P(("groups", "dc", "sp")))

    def whole(q_gen, k_gen, value_generator_rows, w_reward, plan, gen_order):
        rows = q_gen.shape[0] // (mesh.shape["groups"] * mesh.shape["dc"] * mesh.shape["sp"])
        heads = k_gen.shape[1] // HEAD_WIDTH // mesh.shape["tp"]
        fits = (
            mesh.shape["dc"] in (2, 4)
            and mesh.shape["sp"] == 2
            and heads % 2 == 0
            and rows == HEAD_WIDTH
            and rows % (16 * mesh.shape["dc"] * mesh.shape["sp"]) == 0
        )
        inner = gather_body if fits else body
        return jax.shard_map(inner, mesh=mesh, in_specs=in_specs, out_specs=out_specs, check_vma=False)(
            q_gen, k_gen, value_generator_rows, w_reward, plan, gen_order
        )

    return whole
```

```python
import functools

import jax
import jax.numpy as jnp
from jax import lax
from jax.experimental import pallas as pl
from jax.experimental.pallas import tpu as pltpu
from jax.sharding import PartitionSpec as P

HEAD_WIDTH = 128


NEG = -1e30


def from_behind(block, axis, distance):
    devices = range(lax.axis_size(axis))
    route = [(i - distance, i) for i in devices if i - distance in devices]
    return lax.ppermute(block, axis, route)


def fold_block(state, key_rows, value_rows, query_rows, allowed, scale):
    top, total, mixed = state
    scores = (
        jnp.einsum("rjge,nje->jgrn", query_rows, key_rows, preferred_element_type=jnp.float32)
        * scale
    )
    if allowed is not None:
        scores = jnp.where(allowed, scores, NEG)
    newtop = jnp.maximum(top, jnp.max(scores, axis=-1))
    shrink = jnp.exp(top - newtop)
    weight = jnp.exp(scores - newtop[..., None])
    if allowed is not None:
        weight = jnp.where(allowed, weight, 0.0)
    total = total * shrink + jnp.sum(weight, axis=-1)
    update = jnp.einsum(
        "jgrn,nje->jgre",
        weight.astype(jnp.bfloat16),
        value_rows,
        preferred_element_type=jnp.float32,
    )
    return (newtop, total, mixed * shrink[..., None] + update)


def body(q_gen, k_gen, value_generator_rows, w_reward, plan, gen_order):
    ranks = lax.axis_size(("dc", "sp"))
    sp_size = lax.axis_size("sp")
    dc_size = ranks // sp_size
    rows = q_gen.shape[0]
    piece = rows // ranks
    width_q = q_gen.shape[1]
    width_kv = k_gen.shape[1]
    heads_kv = width_kv // HEAD_WIDTH
    rollout_group = width_q // HEAD_WIDTH // heads_kv
    scale = HEAD_WIDTH ** (-0.5)
    order_row = gen_order[0]
    labels = jnp.arange(ranks, dtype=jnp.int32)
    inverse = jnp.sum(jnp.where(order_row[:, None] == labels[None, :], labels[:, None], 0), axis=0)
    q_send = jnp.take(q_gen.reshape(ranks, piece, width_q), inverse, axis=0)
    k_send = jnp.take(k_gen.reshape(ranks, piece, width_kv), inverse, axis=0)
    v_send = jnp.take(value_generator_rows.reshape(ranks, piece, width_kv), inverse, axis=0)
    q_flat = q_send.reshape(rows, width_q)
    k_flat = k_send.reshape(rows, width_kv)
    v_flat = v_send.reshape(rows, width_kv)
    query_layout, key_layout, value_layout = (
        lax.all_to_all(q_flat, ("dc", "sp"), split_axis=0, concat_axis=0, tiled=True),
        lax.all_to_all(k_flat, ("dc", "sp"), split_axis=0, concat_axis=0, tiled=True),
        lax.all_to_all(v_flat, ("dc", "sp"), split_axis=0, concat_axis=0, tiled=True),
    )
    me = lax.axis_index(("dc", "sp"))
    my_dc = me // sp_size
    start = plan[0, my_dc]
    length = plan[2, my_dc]
    local = jnp.arange(rows, dtype=jnp.int32)
    position = (my_dc - start) * (rows * sp_size) + me % sp_size * rows + local
    valid = position < length
    query_rows = query_layout.reshape(rows, heads_kv, rollout_group, HEAD_WIDTH)
    state = (
        jnp.full((heads_kv, rollout_group, rows), NEG, jnp.float32),
        jnp.zeros((heads_kv, rollout_group, rows), jnp.float32),
        jnp.zeros((heads_kv, rollout_group, rows, HEAD_WIDTH), jnp.float32),
    )
    causal = local[None, :] <= local[:, None]
    state = fold_block(
        state,
        key_layout.reshape(rows, heads_kv, HEAD_WIDTH),
        value_layout.reshape(rows, heads_kv, HEAD_WIDTH),
        query_rows,
        causal,
        scale,
    )
    own = jnp.stack([key_layout, value_layout])
    reach = max(dc_size // 2, 1) * sp_size

    def advance(step, carry):
        folded, moving = carry
        moving = from_behind(moving, ("dc", "sp"), 1)
        source = me - step - 1
        use = (source >= 0) & (source // sp_size >= start)
        folded = lax.cond(
            use,
            lambda carried: fold_block(
                carried,
                moving[0].reshape(rows, heads_kv, HEAD_WIDTH),
                moving[1].reshape(rows, heads_kv, HEAD_WIDTH),
                query_rows,
                None,
                scale,
            ),
            lambda carried: carried,
            folded,
        )
        return (folded, moving)

    state, _ = lax.fori_loop(0, reach - 1, advance, (state, own))
    top, total, mixed = state
    hidden = mixed / total[..., None]
    hidden = jnp.transpose(hidden, (2, 0, 1, 3)).reshape(rows, width_q)
    hidden = jnp.where(valid[:, None], hidden, 0.0).astype(jnp.bfloat16)
    back = lax.all_to_all(hidden, ("dc", "sp"), split_axis=0, concat_axis=0, tiled=True)
    scored = jnp.take(back.reshape(ranks, piece, width_q), order_row, axis=0).reshape(rows, width_q)
    partial_reward = jnp.sum(scored.astype(jnp.float32) * w_reward[None, :], axis=1)
    reward = lax.psum(partial_reward, "tp")
    return (scored, reward)


MESH = pl.DeviceIdType.MESH
BIG = -1e30


def gather_attend(
    sizes, order_hbm, plan_hbm, q_hbm, k_hbm, v_hbm, w_hbm, out_ref, rew_ref, order_out,
    order_ref, plan_ref, q_ref, k_ref, v_ref, w_ref, q_send, q_all, kv_send, kv_all, hid_send, racc, rew_all,
    kv_ssem, kv_rsem, fwd_ssem, q_ssem, q_rsem, hid_ssem, hid_rsem, rew_ssem, rew_rsem, in_sem,
):
    dcs, sps, tps, piece, rows, heads, group, jc, span, halves = sizes
    ranks, units, width = dcs * sps, jc * halves, group * HEAD_WIDTH
    dc, sp, tp = lax.axis_index("dc"), lax.axis_index("sp"), lax.axis_index("tp")
    me, other = dc * sps + sp, 1 - sp

    arguments = ((order_hbm, order_ref), (k_hbm, k_ref), (v_hbm, v_ref), (q_hbm, q_ref), (plan_hbm, plan_ref), (w_hbm, w_ref))
    loads = [pltpu.make_async_copy(a, b, in_sem.at[i]) for i, (a, b) in enumerate(arguments)]
    for load in loads:
        load.start()

    barrier = pltpu.get_barrier_semaphore()
    for rank in range(ranks):
        @pl.when(rank != me)
        def _():
            pl.semaphore_signal(
                barrier, inc=1, device_id={"dc": rank // sps, "sp": rank % sps}, device_id_type=MESH
            )
    for shift in range(1, tps):
        for core in range(sps):
            pl.semaphore_signal(
                barrier, inc=1, device_id={"tp": lax.rem(tp + shift, tps), "sp": core}, device_id_type=MESH
            )

    for load in loads[:3]:
        load.wait()
    segments = []
    for d in range(ranks):
        seg = jnp.int32(0)
        for s in range(1, ranks):
            seg = jnp.where(order_ref[0, s] == d, s, seg)
        segments.append(seg)
    for d in range(ranks):
        h, dl = d // span, d % span
        for jj in range(jc):
            u = jj * halves + h
            for core in range(sps):
                cols = pl.ds((core * jc + jj) * HEAD_WIDTH, HEAD_WIDTH)
                kv_send[core, u, 0, pl.ds(dl * piece, piece), :] = k_ref[segments[d], :, cols]
                kv_send[core, u, 1, pl.ds(dl * piece, piece), :] = v_ref[segments[d], :, cols]

    pl.semaphore_wait(barrier, ranks - 1 + (tps - 1) * sps)

    steps = [sign * hop for hop in (1, 2) if hop < dcs for sign in (1, -1)]

    def direct(step):
        target = dc + step
        inside = (target >= 0) & (target < dcs)
        return inside if abs(step) == 1 else inside & (target > 0) & (target < dcs - 1)

    relays = ((1, (2, 3), 0), (2, (1, 0), 3)) if dcs == 4 else ()

    def kv_copy(u, i, core):
        return pltpu.make_async_remote_copy(
            src_ref=kv_send.at[core, u], dst_ref=kv_all.at[u, me],
            send_sem=kv_ssem.at[u, i * sps + core], recv_sem=kv_rsem.at[u, me],
            device_id={"dc": dc + steps[i], "sp": core}, device_id_type=MESH,
        )

    def kv_copy_sibling(u):
        return pltpu.make_async_remote_copy(
            src_ref=kv_send.at[other, u], dst_ref=kv_all.at[u, me],
            send_sem=kv_ssem.at[u, len(steps) * sps], recv_sem=kv_rsem.at[u, me],
            device_id={"sp": other}, device_id_type=MESH,
        )

    def kv_forward(u, k, core, source_dc, target_dc):
        source = source_dc * sps + core
        return pltpu.make_async_remote_copy(
            src_ref=kv_all.at[u, source], dst_ref=kv_all.at[u, source],
            send_sem=fwd_ssem.at[u, k * sps + core], recv_sem=kv_rsem.at[u, source],
            device_id={"dc": target_dc}, device_id_type=MESH,
        )

    def kv_wait(u, source):
        pltpu.make_async_remote_copy(
            src_ref=kv_all.at[u, source], dst_ref=kv_all.at[u, source],
            send_sem=kv_ssem.at[u, 0], recv_sem=kv_rsem.at[u, source],
            device_id={"sp": other}, device_id_type=MESH,
        ).wait_recv()

    q_copy = pltpu.make_async_remote_copy(
        src_ref=q_send, dst_ref=q_all.at[1], send_sem=q_ssem, recv_sem=q_rsem,
        device_id={"sp": other}, device_id_type=MESH,
    )

    def send_unit(u, carry):
        for i, step in enumerate(steps):
            @pl.when(direct(step))
            def _():
                for core in range(sps):
                    kv_copy(u, i, core).start()
        kv_copy_sibling(u).start()
        kv_all[u, me] = kv_send[sp, u]
        return carry

    lax.fori_loop(0, units, send_unit, 0)
    loads[3].wait()
    for d in range(ranks):
        h, dl = d // span, d % span
        for jj in range(jc):
            u = jj * halves + h
            mine = pl.ds(pl.multiple_of((sp * jc + jj) * width, width), width)
            theirs = pl.ds(pl.multiple_of((other * jc + jj) * width, width), width)
            q_send[u, dl] = q_ref[segments[d], :, theirs]
            q_all[0, u, dl] = q_ref[segments[d], :, mine]
    q_copy.start()
    for load in loads[4:]:
        load.wait()

    tile = 2 * group * piece
    row = lax.broadcasted_iota(jnp.int32, (tile, 1), 0)
    rank_of_row = dc * sps + jnp.where(row < group * piece, sp, other)
    offset = rank_of_row * piece + lax.rem(row, piece)
    column = lax.broadcasted_iota(jnp.int32, (tile, rows), 1)
    causal = jnp.where(column <= offset, 0.0, BIG)
    factor = HEAD_WIDTH ** (-0.5) * 1.4426950408889634

    def hid_place(u):
        head = sp * jc + u // halves
        return out_ref.at[
            pl.ds(lax.rem(u, halves) * span, span), :, pl.ds(pl.multiple_of(head * width, width), width)
        ]

    def hid_copy(u):
        return pltpu.make_async_remote_copy(
            src_ref=hid_send.at[u], dst_ref=hid_place(u),
            send_sem=hid_ssem.at[u], recv_sem=hid_rsem.at[u],
            device_id={"sp": other}, device_id_type=MESH,
        )

    q_copy.wait_recv()

    def attend(u, carry):
        jj, h = u // halves, lax.rem(u, halves)
        head = sp * jc + jj
        for relay, fars, end in relays:
            @pl.when(dc == relay)
            def _():
                for k, far in enumerate(fars):
                    for core in range(sps):
                        kv_wait(u, far * sps + core)
                        kv_forward(u, k, core, far, end).start()
        for source in range(ranks):
            waits = source != me
            for relay, fars, _ in relays:
                if source // sps in fars:
                    waits = waits & (dc != relay)

            @pl.when(waits)
            def _():
                kv_wait(u, source)

        def plan_order(which):
            return jnp.concatenate(
                [
                    kv_all[u, source, which, pl.ds(dl * piece, piece), :]
                    for dl in range(span)
                    for source in range(ranks)
                ],
                axis=0,
            )

        keys, values = plan_order(0), plan_order(1)
        for dl in range(span):
            d = h * span + dl
            slot = d // sps
            n = (dl + 1) * rows
            query = jnp.concatenate(
                [
                    q_all[t, u, dl, :, pl.ds(g * HEAD_WIDTH, HEAD_WIDTH)]
                    for t in range(2)
                    for g in range(group)
                ],
                axis=0,
            )
            scores = lax.dot_general(
                query, keys[:n], (((1,), (1,)), ((), ())), preferred_element_type=jnp.float32
            )
            start = plan_ref[0, slot]
            blocks = []
            for d2 in range(dl + 1):
                block = scores[:, d2 * rows:(d2 + 1) * rows]
                if d2 == dl:
                    block = block + causal
                elif d2 // sps != dl // sps:
                    block = block + jnp.where(plan_ref[0, h * (span // sps) + d2 // sps] == start, 0.0, BIG)
                blocks.append(block)
            peak = blocks[0]
            for block in blocks[1:]:
                peak = jnp.maximum(peak, block)
            top = jnp.max(peak, axis=1, keepdims=True)
            weights = [jnp.exp2((block - top) * factor) for block in blocks]
            total = weights[0]
            for weight in weights[1:]:
                total = total + weight
            total = jnp.sum(total, axis=1, keepdims=True)
            weight16 = jnp.concatenate([weight.astype(jnp.bfloat16) for weight in weights], axis=1)
            mixed = jnp.dot(weight16, values[:n], preferred_element_type=jnp.float32)
            base = (slot - start) * (rows * sps) + lax.rem(d, sps) * rows
            share = jnp.where(offset + base < plan_ref[2, slot], 1.0 / total, 0.0)
            hidden = (mixed * share).astype(jnp.bfloat16)
            for t in range(2):
                reward = jnp.zeros((piece, HEAD_WIDTH), jnp.float32)
                for g in range(group):
                    part = hidden[(t * group + g) * piece:(t * group + g + 1) * piece]
                    cols = pl.ds(g * HEAD_WIDTH, HEAD_WIDTH)
                    if t == 0:
                        out_ref[d, :, pl.ds(pl.multiple_of(head * width, width) + g * HEAD_WIDTH, HEAD_WIDTH)] = part
                    else:
                        hid_send[u, dl, :, cols] = part
                    w = w_ref[sp * jc + jj, pl.ds(g, 1), :]
                    reward = reward + part.astype(jnp.float32) * w
                racc[u, t, pl.ds(dl * piece, piece), :] = reward
        hid_copy(u).start()
        return carry

    lax.fori_loop(0, units, attend, 0)

    sums = []
    for t in range(2):
        cells = []
        for h in range(halves):
            cell = racc[h, t]
            for jj in range(1, jc):
                cell = cell + racc[jj * halves + h, t]
            cells.append(cell)
        line = jnp.sum(jnp.concatenate(cells, axis=0).T, axis=0, keepdims=True)
        sums.append(jnp.broadcast_to(line, (8, rows)))
    slot_me = tp * sps + sp
    rew_all[tps * sps] = sums[1]
    rew_all[slot_me] = sums[0]

    def rew_copy(shift, same):
        peer = lax.rem(tp + shift, tps)
        return pltpu.make_async_remote_copy(
            src_ref=rew_all.at[slot_me if same else tps * sps], dst_ref=rew_all.at[slot_me],
            send_sem=rew_ssem.at[2 * shift + (0 if same else 1)], recv_sem=rew_rsem.at[slot_me],
            device_id={"tp": peer, "sp": sp if same else other}, device_id_type=MESH,
        )

    pairs = [(shift, same) for shift in range(tps) for same in (True, False) if (shift, same) != (0, True)]
    for shift, same in pairs:
        rew_copy(shift, same).start()

    for source in range(tps * sps):
        @pl.when(source != slot_me)
        def _():
            pltpu.make_async_remote_copy(
                src_ref=rew_all.at[source], dst_ref=rew_all.at[source],
                send_sem=rew_ssem.at[0], recv_sem=rew_rsem.at[source],
                device_id={"sp": other}, device_id_type=MESH,
            ).wait_recv()
    reward = rew_all[0]
    for source in range(1, tps * sps):
        reward = reward + rew_all[source]
    rew_ref[...] = reward
    for s in range(ranks):
        order_out[0, s] = order_ref[0, s]

    for shift, same in pairs:
        rew_copy(shift, same).wait_send()
    q_copy.wait_send()

    def drain(u, carry):
        hid_copy(u).wait()
        kv_copy_sibling(u).wait_send()
        for i, step in enumerate(steps):
            @pl.when(direct(step))
            def _():
                for core in range(sps):
                    kv_copy(u, i, core).wait_send()
        for relay, fars, end in relays:
            @pl.when(dc == relay)
            def _():
                for k, far in enumerate(fars):
                    for core in range(sps):
                        kv_forward(u, k, core, far, end).wait_send()
        return carry

    lax.fori_loop(0, units, drain, 0)


def to_generator_order(ranks, piece, order_ref, hidden, reward_ref, out, out_reward, line, sems):
    copies = [
        pltpu.make_async_copy(hidden.at[order_ref[0, s]], out.at[pl.ds(s * piece, piece)], sems.at[s])
        for s in range(ranks)
    ]
    for copy in copies:
        copy.start()
    reward = reward_ref[...]
    segment = lax.broadcasted_iota(jnp.int32, reward.shape, 1) // piece
    moved = reward
    for s in range(ranks):
        shift = lax.rem(s - order_ref[0, s] + ranks, ranks) * piece
        moved = jnp.where(segment == s, pltpu.roll(reward, shift, 1), moved)
    line[...] = moved[:1]
    last = pltpu.make_async_copy(line, out_reward, sems.at[ranks])
    last.start()
    for copy in copies + [last]:
        copy.wait()


def gather_body(q_gen, k_gen, value_generator_rows, w_reward, plan, gen_order):
    dcs, sps, tps = lax.axis_size("dc"), lax.axis_size("sp"), lax.axis_size("tp")
    ranks = dcs * sps
    rows, width_q = q_gen.shape
    width_kv = k_gen.shape[1]
    piece = rows // ranks
    heads = width_kv // HEAD_WIDTH
    group = width_q // width_kv
    jc = heads // sps
    span = max(dcs // 2, 1) * sps
    halves = ranks // span
    units, width = jc * halves, group * HEAD_WIDTH
    sizes = (dcs, sps, tps, piece, rows, heads, group, jc, span, halves)
    bf16, f32 = jnp.bfloat16, jnp.float32
    vmem, hbm = pl.BlockSpec(memory_space=pltpu.VMEM), pl.BlockSpec(memory_space=pltpu.HBM)
    smem = pl.BlockSpec(memory_space=pltpu.SMEM)
    dma = pltpu.SemaphoreType.DMA
    hidden, reward, order = pl.pallas_call(
        functools.partial(gather_attend, sizes),
        out_shape=(
            pltpu.VMEM((ranks, piece, width_q), bf16),
            pltpu.VMEM((8, rows), f32),
            pltpu.SMEM(gen_order.shape, jnp.int32),
        ),
        in_specs=[hbm] * 6,
        out_specs=(vmem, vmem, smem),
        scratch_shapes=[
            pltpu.SMEM(gen_order.shape, jnp.int32),
            pltpu.SMEM(plan.shape, jnp.int32),
            pltpu.VMEM((ranks, piece, width_q), bf16),
            pltpu.VMEM((ranks, piece, width_kv), bf16),
            pltpu.VMEM((ranks, piece, width_kv), bf16),
            pltpu.VMEM((heads, group, HEAD_WIDTH), f32),
            pltpu.VMEM((units, span, piece, width), bf16),
            pltpu.VMEM((2, units, span, piece, width), bf16),
            pltpu.VMEM((sps, units, 2, span * piece, HEAD_WIDTH), bf16),
            pltpu.VMEM((units, ranks, 2, span * piece, HEAD_WIDTH), bf16),
            pltpu.VMEM((units, span, piece, width), bf16),
            pltpu.VMEM((units, 2, span * piece, HEAD_WIDTH), f32),
            pltpu.VMEM((tps * sps + 1, 8, rows), f32),
            dma((units, 4 * sps + 1)),
            dma((units, ranks)),
            dma((units, 2 * sps)),
            dma,
            dma,
            dma((units,)),
            dma((units,)),
            dma((2 * tps,)),
            dma((tps * sps,)),
            dma((6,)),
        ],
        compiler_params=pltpu.CompilerParams(
            collective_id=0, has_side_effects=True, vmem_limit_bytes=32 * 1024 * 1024
        ),
    )(*[
        pltpu.with_memory_space_constraint(operand, pltpu.HBM)
        for operand in (
            gen_order,
            plan,
            q_gen.reshape(ranks, piece, width_q),
            k_gen.reshape(ranks, piece, width_kv),
            value_generator_rows.reshape(ranks, piece, width_kv),
            w_reward.reshape(heads, group, HEAD_WIDTH),
        )
    ])
    scored, reward = pl.pallas_call(
        functools.partial(to_generator_order, ranks, piece),
        out_shape=(pltpu.HBM((rows, width_q), bf16), pltpu.HBM((1, rows), f32)),
        in_specs=[smem, vmem, vmem],
        out_specs=(hbm, hbm),
        scratch_shapes=[pltpu.VMEM((1, rows), f32), dma((ranks + 1,))],
    )(order, pltpu.with_memory_space_constraint(hidden, pltpu.VMEM), pltpu.with_memory_space_constraint(reward, pltpu.VMEM))
    return (scored, reward.reshape(rows))


def solution(mesh):
    in_specs = (
        P(("groups", "dc", "sp"), "tp"),
        P(("groups", "dc", "sp"), "tp"),
        P(("groups", "dc", "sp"), "tp"),
        P("tp"),
        P(None, "groups"),
        P(("groups", "dc", "sp"), None),
    )
    out_specs = (P(("groups", "dc", "sp"), "tp"), P(("groups", "dc", "sp")))

    def whole(q_gen, k_gen, value_generator_rows, w_reward, plan, gen_order):
        rows = q_gen.shape[0] // (mesh.shape["groups"] * mesh.shape["dc"] * mesh.shape["sp"])
        heads = k_gen.shape[1] // HEAD_WIDTH // mesh.shape["tp"]
        fits = (
            mesh.shape["dc"] in (2, 4)
            and mesh.shape["sp"] == 2
            and heads % 2 == 0
            and rows == HEAD_WIDTH
            and rows % (16 * mesh.shape["dc"] * mesh.shape["sp"]) == 0
        )
        inner = gather_body if fits else body
        return jax.shard_map(inner, mesh=mesh, in_specs=in_specs, out_specs=out_specs, check_vma=False)(
            q_gen, k_gen, value_generator_rows, w_reward, plan, gen_order
        )

    return whole
```

```python
import functools

import jax
import jax.numpy as jnp
from jax import lax
from jax.experimental import pallas as pl
from jax.experimental.pallas import tpu as pltpu
from jax.sharding import PartitionSpec as P

HEAD_WIDTH = 128


NEG = -1e30


def from_behind(block, axis, distance):
    devices = range(lax.axis_size(axis))
    route = [(i - distance, i) for i in devices if i - distance in devices]
    return lax.ppermute(block, axis, route)


def fold_block(state, key_rows, value_rows, query_rows, allowed, scale):
    top, total, mixed = state
    scores = (
        jnp.einsum("rjge,nje->jgrn", query_rows, key_rows, preferred_element_type=jnp.float32)
        * scale
    )
    if allowed is not None:
        scores = jnp.where(allowed, scores, NEG)
    newtop = jnp.maximum(top, jnp.max(scores, axis=-1))
    shrink = jnp.exp(top - newtop)
    weight = jnp.exp(scores - newtop[..., None])
    if allowed is not None:
        weight = jnp.where(allowed, weight, 0.0)
    total = total * shrink + jnp.sum(weight, axis=-1)
    update = jnp.einsum(
        "jgrn,nje->jgre",
        weight.astype(jnp.bfloat16),
        value_rows,
        preferred_element_type=jnp.float32,
    )
    return (newtop, total, mixed * shrink[..., None] + update)


def body(q_gen, k_gen, value_generator_rows, w_reward, plan, gen_order):
    ranks = lax.axis_size(("dc", "sp"))
    sp_size = lax.axis_size("sp")
    dc_size = ranks // sp_size
    rows = q_gen.shape[0]
    piece = rows // ranks
    width_q = q_gen.shape[1]
    width_kv = k_gen.shape[1]
    heads_kv = width_kv // HEAD_WIDTH
    rollout_group = width_q // HEAD_WIDTH // heads_kv
    scale = HEAD_WIDTH ** (-0.5)
    order_row = gen_order[0]
    labels = jnp.arange(ranks, dtype=jnp.int32)
    inverse = jnp.sum(jnp.where(order_row[:, None] == labels[None, :], labels[:, None], 0), axis=0)
    q_send = jnp.take(q_gen.reshape(ranks, piece, width_q), inverse, axis=0)
    k_send = jnp.take(k_gen.reshape(ranks, piece, width_kv), inverse, axis=0)
    v_send = jnp.take(value_generator_rows.reshape(ranks, piece, width_kv), inverse, axis=0)
    q_flat = q_send.reshape(rows, width_q)
    k_flat = k_send.reshape(rows, width_kv)
    v_flat = v_send.reshape(rows, width_kv)
    query_layout, key_layout, value_layout = (
        lax.all_to_all(q_flat, ("dc", "sp"), split_axis=0, concat_axis=0, tiled=True),
        lax.all_to_all(k_flat, ("dc", "sp"), split_axis=0, concat_axis=0, tiled=True),
        lax.all_to_all(v_flat, ("dc", "sp"), split_axis=0, concat_axis=0, tiled=True),
    )
    me = lax.axis_index(("dc", "sp"))
    my_dc = me // sp_size
    start = plan[0, my_dc]
    length = plan[2, my_dc]
    local = jnp.arange(rows, dtype=jnp.int32)
    position = (my_dc - start) * (rows * sp_size) + me % sp_size * rows + local
    valid = position < length
    query_rows = query_layout.reshape(rows, heads_kv, rollout_group, HEAD_WIDTH)
    state = (
        jnp.full((heads_kv, rollout_group, rows), NEG, jnp.float32),
        jnp.zeros((heads_kv, rollout_group, rows), jnp.float32),
        jnp.zeros((heads_kv, rollout_group, rows, HEAD_WIDTH), jnp.float32),
    )
    causal = local[None, :] <= local[:, None]
    state = fold_block(
        state,
        key_layout.reshape(rows, heads_kv, HEAD_WIDTH),
        value_layout.reshape(rows, heads_kv, HEAD_WIDTH),
        query_rows,
        causal,
        scale,
    )
    own = jnp.stack([key_layout, value_layout])
    reach = max(dc_size // 2, 1) * sp_size

    def advance(step, carry):
        folded, moving = carry
        moving = from_behind(moving, ("dc", "sp"), 1)
        source = me - step - 1
        use = (source >= 0) & (source // sp_size >= start)
        folded = lax.cond(
            use,
            lambda carried: fold_block(
                carried,
                moving[0].reshape(rows, heads_kv, HEAD_WIDTH),
                moving[1].reshape(rows, heads_kv, HEAD_WIDTH),
                query_rows,
                None,
                scale,
            ),
            lambda carried: carried,
            folded,
        )
        return (folded, moving)

    state, _ = lax.fori_loop(0, reach - 1, advance, (state, own))
    top, total, mixed = state
    hidden = mixed / total[..., None]
    hidden = jnp.transpose(hidden, (2, 0, 1, 3)).reshape(rows, width_q)
    hidden = jnp.where(valid[:, None], hidden, 0.0).astype(jnp.bfloat16)
    back = lax.all_to_all(hidden, ("dc", "sp"), split_axis=0, concat_axis=0, tiled=True)
    scored = jnp.take(back.reshape(ranks, piece, width_q), order_row, axis=0).reshape(rows, width_q)
    partial_reward = jnp.sum(scored.astype(jnp.float32) * w_reward[None, :], axis=1)
    reward = lax.psum(partial_reward, "tp")
    return (scored, reward)


MESH = pl.DeviceIdType.MESH
BIG = -1e30


def gather_attend(
    sizes, order_hbm, plan_hbm, q_hbm, k_hbm, v_hbm, w_hbm, out_ref, rew_ref, order_out,
    order_ref, plan_ref, q_ref, k_ref, v_ref, w_ref, q_send, q_all, kv_send, kv_all, hid_send, racc, rew_all,
    kv_ssem, kv_rsem, fwd_ssem, q_ssem, q_rsem, hid_ssem, hid_rsem, rew_ssem, rew_rsem, in_sem,
):
    dcs, sps, tps, piece, rows, heads, group, jc, span, halves = sizes
    ranks, units, width = dcs * sps, jc * halves, group * HEAD_WIDTH
    dc, sp, tp = lax.axis_index("dc"), lax.axis_index("sp"), lax.axis_index("tp")
    me, other = dc * sps + sp, 1 - sp

    arguments = ((order_hbm, order_ref), (k_hbm, k_ref), (v_hbm, v_ref), (q_hbm, q_ref), (plan_hbm, plan_ref), (w_hbm, w_ref))
    loads = [pltpu.make_async_copy(a, b, in_sem.at[i]) for i, (a, b) in enumerate(arguments)]
    for load in loads:
        load.start()

    barrier = pltpu.get_barrier_semaphore()
    for rank in range(ranks):
        @pl.when(rank != me)
        def _():
            pl.semaphore_signal(
                barrier, inc=1, device_id={"dc": rank // sps, "sp": rank % sps}, device_id_type=MESH
            )
    for shift in range(1, tps):
        for core in range(sps):
            pl.semaphore_signal(
                barrier, inc=1, device_id={"tp": lax.rem(tp + shift, tps), "sp": core}, device_id_type=MESH
            )

    for load in loads[:3]:
        load.wait()
    segments = []
    for d in range(ranks):
        seg = jnp.int32(0)
        for s in range(1, ranks):
            seg = jnp.where(order_ref[0, s] == d, s, seg)
        segments.append(seg)
    for d in range(ranks):
        h, dl = d // span, d % span
        for jj in range(jc):
            u = jj * halves + h
            for core in range(sps):
                cols = pl.ds((core * jc + jj) * HEAD_WIDTH, HEAD_WIDTH)
                kv_send[core, u, 0, pl.ds(dl * piece, piece), :] = k_ref[segments[d], :, cols]
                kv_send[core, u, 1, pl.ds(dl * piece, piece), :] = v_ref[segments[d], :, cols]

    pl.semaphore_wait(barrier, ranks - 1 + (tps - 1) * sps)

    steps = [sign * hop for hop in (1, 2) if hop < dcs for sign in (1, -1)]

    def direct(step):
        target = dc + step
        inside = (target >= 0) & (target < dcs)
        return inside if abs(step) == 1 else inside & (target > 0) & (target < dcs - 1)

    relays = ((1, (2, 3), 0), (2, (1, 0), 3)) if dcs == 4 else ()

    def cut(ref, *index, part):
        return ref.at[index if part is None else index + (part,)]

    def kv_copy(u, i, core, part):
        return pltpu.make_async_remote_copy(
            src_ref=cut(kv_send, core, u, part=part), dst_ref=cut(kv_all, u, me, part=part),
            send_sem=kv_ssem.at[u, part or 0, i * sps + core], recv_sem=kv_rsem.at[u, part or 0, me],
            device_id={"dc": dc + steps[i], "sp": core}, device_id_type=MESH,
        )

    def kv_copy_sibling(u, part):
        return pltpu.make_async_remote_copy(
            src_ref=cut(kv_send, other, u, part=part), dst_ref=cut(kv_all, u, me, part=part),
            send_sem=kv_ssem.at[u, part or 0, len(steps) * sps], recv_sem=kv_rsem.at[u, part or 0, me],
            device_id={"sp": other}, device_id_type=MESH,
        )

    def kv_forward(u, k, core, source_dc, target_dc, part):
        source = source_dc * sps + core
        return pltpu.make_async_remote_copy(
            src_ref=cut(kv_all, u, source, part=part), dst_ref=cut(kv_all, u, source, part=part),
            send_sem=fwd_ssem.at[u, part or 0, k * sps + core], recv_sem=kv_rsem.at[u, part or 0, source],
            device_id={"dc": target_dc}, device_id_type=MESH,
        )

    def kv_wait(u, source, part):
        pltpu.make_async_remote_copy(
            src_ref=cut(kv_all, u, source, part=part), dst_ref=cut(kv_all, u, source, part=part),
            send_sem=kv_ssem.at[u, part or 0, 0], recv_sem=kv_rsem.at[u, part or 0, source],
            device_id={"sp": other}, device_id_type=MESH,
        ).wait_recv()

    q_copy = pltpu.make_async_remote_copy(
        src_ref=q_send, dst_ref=q_all.at[1], send_sem=q_ssem, recv_sem=q_rsem,
        device_id={"sp": other}, device_id_type=MESH,
    )

    def send_unit(u, part):
        for i, step in enumerate(steps):
            @pl.when(direct(step))
            def _():
                for core in range(sps):
                    kv_copy(u, i, core, part).start()
        kv_copy_sibling(u, part).start()

    last = units - 1

    def send_whole(u, carry):
        send_unit(u, None)
        return carry

    lax.fori_loop(0, last, send_whole, 0)
    for part in range(2):
        send_unit(last, part)
    for u in range(units):
        kv_all[u, me] = kv_send[sp, u]
    loads[3].wait()
    for d in range(ranks):
        h, dl = d // span, d % span
        for jj in range(jc):
            u = jj * halves + h
            mine = pl.ds(pl.multiple_of((sp * jc + jj) * width, width), width)
            theirs = pl.ds(pl.multiple_of((other * jc + jj) * width, width), width)
            q_send[u, dl] = q_ref[segments[d], :, theirs]
            q_all[0, u, dl] = q_ref[segments[d], :, mine]
    q_copy.start()
    for load in loads[4:]:
        load.wait()

    tile = 2 * group * piece
    row = lax.broadcasted_iota(jnp.int32, (tile, 1), 0)
    rank_of_row = dc * sps + jnp.where(row < group * piece, sp, other)
    offset = rank_of_row * piece + lax.rem(row, piece)
    column = lax.broadcasted_iota(jnp.int32, (tile, rows), 1)
    causal = jnp.where(column <= offset, 0.0, BIG)
    factor = HEAD_WIDTH ** (-0.5) * 1.4426950408889634

    def hid_place(u):
        head = sp * jc + u // halves
        return out_ref.at[
            pl.ds(lax.rem(u, halves) * span, span), :, pl.ds(pl.multiple_of(head * width, width), width)
        ]

    def hid_copy(u):
        return pltpu.make_async_remote_copy(
            src_ref=hid_send.at[u], dst_ref=hid_place(u),
            send_sem=hid_ssem.at[u], recv_sem=hid_rsem.at[u],
            device_id={"sp": other}, device_id_type=MESH,
        )

    def pass_on(u, part):
        for relay, fars, end in relays:
            @pl.when(dc == relay)
            def _():
                for k, far in enumerate(fars):
                    for core in range(sps):
                        kv_wait(u, far * sps + core, part)
                        kv_forward(u, k, core, far, end, part).start()

    def arrive(u, part):
        for source in range(ranks):
            waits = source != me
            for relay, fars, _ in relays:
                if source // sps in fars:
                    waits = waits & (dc != relay)

            @pl.when(waits)
            def _():
                kv_wait(u, source, part)

    def attend(u, split):
        jj, h = u // halves, lax.rem(u, halves)
        head = sp * jc + jj

        def plan_order(which):
            return jnp.concatenate(
                [
                    kv_all[u, source, which, pl.ds(dl * piece, piece), :]
                    for dl in range(span)
                    for source in range(ranks)
                ],
                axis=0,
            )

        arrive(u, 0 if split else None)
        keys = plan_order(0)
        weighed = []
        for dl in range(span):
            d = h * span + dl
            slot = d // sps
            n = (dl + 1) * rows
            query = jnp.concatenate(
                [
                    q_all[t, u, dl, :, pl.ds(g * HEAD_WIDTH, HEAD_WIDTH)]
                    for t in range(2)
                    for g in range(group)
                ],
                axis=0,
            )
            scores = lax.dot_general(
                query, keys[:n], (((1,), (1,)), ((), ())), preferred_element_type=jnp.float32
            )
            start = plan_ref[0, slot]
            blocks = []
            for d2 in range(dl + 1):
                block = scores[:, d2 * rows:(d2 + 1) * rows]
                if d2 == dl:
                    block = block + causal
                elif d2 // sps != dl // sps:
                    block = block + jnp.where(plan_ref[0, h * (span // sps) + d2 // sps] == start, 0.0, BIG)
                blocks.append(block)
            peak = blocks[0]
            for block in blocks[1:]:
                peak = jnp.maximum(peak, block)
            top = jnp.max(peak, axis=1, keepdims=True)
            weights = [jnp.exp2((block - top) * factor) for block in blocks]
            total = weights[0]
            for weight in weights[1:]:
                total = total + weight
            total = jnp.sum(total, axis=1, keepdims=True)
            weight16 = jnp.concatenate([weight.astype(jnp.bfloat16) for weight in weights], axis=1)
            base = (slot - start) * (rows * sps) + lax.rem(d, sps) * rows
            share = jnp.where(offset + base < plan_ref[2, slot], 1.0 / total, 0.0)
            weighed.append((weight16, share))
        if split:
            arrive(u, 1)
        values = plan_order(1)
        for dl, (weight16, share) in enumerate(weighed):
            d = h * span + dl
            mixed = jnp.dot(weight16, values[:(dl + 1) * rows], preferred_element_type=jnp.float32)
            hidden = (mixed * share).astype(jnp.bfloat16)
            for t in range(2):
                reward = jnp.zeros((piece, HEAD_WIDTH), jnp.float32)
                for g in range(group):
                    part = hidden[(t * group + g) * piece:(t * group + g + 1) * piece]
                    cols = pl.ds(g * HEAD_WIDTH, HEAD_WIDTH)
                    if t == 0:
                        out_ref[d, :, pl.ds(pl.multiple_of(head * width, width) + g * HEAD_WIDTH, HEAD_WIDTH)] = part
                    else:
                        hid_send[u, dl, :, cols] = part
                    w = w_ref[sp * jc + jj, pl.ds(g, 1), :]
                    reward = reward + part.astype(jnp.float32) * w
                racc[u, t, pl.ds(dl * piece, piece), :] = reward
        hid_copy(u).start()

    def attend_whole(u, carry):
        attend(u, False)
        return carry

    def pass_on_whole(u, carry):
        pass_on(u, None)
        return carry

    lax.fori_loop(0, last, pass_on_whole, 0)
    for part in range(2):
        pass_on(last, part)
    q_copy.wait_recv()
    lax.fori_loop(0, last, attend_whole, 0)
    attend(jnp.int32(last), True)

    sums = []
    for t in range(2):
        cells = []
        for h in range(halves):
            cell = racc[h, t]
            for jj in range(1, jc):
                cell = cell + racc[jj * halves + h, t]
            cells.append(cell)
        line = jnp.sum(jnp.concatenate(cells, axis=0).T, axis=0, keepdims=True)
        sums.append(jnp.broadcast_to(line, (8, rows)))
    slot_me = tp * sps + sp
    rew_all[tps * sps] = sums[1]
    rew_all[slot_me] = sums[0]

    def rew_copy(shift, same):
        peer = lax.rem(tp + shift, tps)
        return pltpu.make_async_remote_copy(
            src_ref=rew_all.at[slot_me if same else tps * sps], dst_ref=rew_all.at[slot_me],
            send_sem=rew_ssem.at[2 * shift + (0 if same else 1)], recv_sem=rew_rsem.at[slot_me],
            device_id={"tp": peer, "sp": sp if same else other}, device_id_type=MESH,
        )

    pairs = [(shift, same) for shift in reversed(range(tps)) for same in (True, False) if (shift, same) != (0, True)]
    for shift, same in pairs:
        rew_copy(shift, same).start()

    for shift, same in pairs:
        rew_copy(shift, same).wait_send()
    q_copy.wait_send()

    def drain(u, part):
        kv_copy_sibling(u, part).wait_send()
        for i, step in enumerate(steps):
            @pl.when(direct(step))
            def _():
                for core in range(sps):
                    kv_copy(u, i, core, part).wait_send()
        for relay, fars, end in relays:
            @pl.when(dc == relay)
            def _():
                for k, far in enumerate(fars):
                    for core in range(sps):
                        kv_forward(u, k, core, far, end, part).wait_send()

    def drain_whole(u, carry):
        drain(u, None)
        return carry

    lax.fori_loop(0, last, drain_whole, 0)
    for part in range(2):
        drain(last, part)
    for u in range(units):
        hid_copy(u).wait()

    for source in range(tps * sps):
        @pl.when(source != slot_me)
        def _():
            pltpu.make_async_remote_copy(
                src_ref=rew_all.at[source], dst_ref=rew_all.at[source],
                send_sem=rew_ssem.at[0], recv_sem=rew_rsem.at[source],
                device_id={"sp": other}, device_id_type=MESH,
            ).wait_recv()
    reward = rew_all[0]
    for source in range(1, tps * sps):
        reward = reward + rew_all[source]
    rew_ref[...] = reward
    for s in range(ranks):
        order_out[0, s] = order_ref[0, s]


def to_generator_order(ranks, piece, order_ref, hidden, reward_ref, out, out_reward, line, sems):
    copies = [
        pltpu.make_async_copy(hidden.at[order_ref[0, s]], out.at[pl.ds(s * piece, piece)], sems.at[s])
        for s in range(ranks)
    ]
    for copy in copies:
        copy.start()
    reward = reward_ref[...]
    segment = lax.broadcasted_iota(jnp.int32, reward.shape, 1) // piece
    moved = reward
    for s in range(ranks):
        shift = lax.rem(s - order_ref[0, s] + ranks, ranks) * piece
        moved = jnp.where(segment == s, pltpu.roll(reward, shift, 1), moved)
    line[...] = moved[:1]
    last = pltpu.make_async_copy(line, out_reward, sems.at[ranks])
    last.start()
    for copy in copies + [last]:
        copy.wait()


def gather_body(q_gen, k_gen, value_generator_rows, w_reward, plan, gen_order):
    dcs, sps, tps = lax.axis_size("dc"), lax.axis_size("sp"), lax.axis_size("tp")
    ranks = dcs * sps
    rows, width_q = q_gen.shape
    width_kv = k_gen.shape[1]
    piece = rows // ranks
    heads = width_kv // HEAD_WIDTH
    group = width_q // width_kv
    jc = heads // sps
    span = max(dcs // 2, 1) * sps
    halves = ranks // span
    units, width = jc * halves, group * HEAD_WIDTH
    sizes = (dcs, sps, tps, piece, rows, heads, group, jc, span, halves)
    bf16, f32 = jnp.bfloat16, jnp.float32
    vmem, hbm = pl.BlockSpec(memory_space=pltpu.VMEM), pl.BlockSpec(memory_space=pltpu.HBM)
    smem = pl.BlockSpec(memory_space=pltpu.SMEM)
    dma = pltpu.SemaphoreType.DMA
    hidden, reward, order = pl.pallas_call(
        functools.partial(gather_attend, sizes),
        out_shape=(
            pltpu.VMEM((ranks, piece, width_q), bf16),
            pltpu.VMEM((8, rows), f32),
            pltpu.SMEM(gen_order.shape, jnp.int32),
        ),
        in_specs=[hbm] * 6,
        out_specs=(vmem, vmem, smem),
        scratch_shapes=[
            pltpu.SMEM(gen_order.shape, jnp.int32),
            pltpu.SMEM(plan.shape, jnp.int32),
            pltpu.VMEM((ranks, piece, width_q), bf16),
            pltpu.VMEM((ranks, piece, width_kv), bf16),
            pltpu.VMEM((ranks, piece, width_kv), bf16),
            pltpu.VMEM((heads, group, HEAD_WIDTH), f32),
            pltpu.VMEM((units, span, piece, width), bf16),
            pltpu.VMEM((2, units, span, piece, width), bf16),
            pltpu.VMEM((sps, units, 2, span * piece, HEAD_WIDTH), bf16),
            pltpu.VMEM((units, ranks, 2, span * piece, HEAD_WIDTH), bf16),
            pltpu.VMEM((units, span, piece, width), bf16),
            pltpu.VMEM((units, 2, span * piece, HEAD_WIDTH), f32),
            pltpu.VMEM((tps * sps + 1, 8, rows), f32),
            dma((units, 2, 4 * sps + 1)),
            dma((units, 2, ranks)),
            dma((units, 2, 2 * sps)),
            dma,
            dma,
            dma((units,)),
            dma((units,)),
            dma((2 * tps,)),
            dma((tps * sps,)),
            dma((6,)),
        ],
        compiler_params=pltpu.CompilerParams(
            collective_id=0, has_side_effects=True, vmem_limit_bytes=32 * 1024 * 1024
        ),
    )(*[
        pltpu.with_memory_space_constraint(operand, pltpu.HBM)
        for operand in (
            gen_order,
            plan,
            q_gen.reshape(ranks, piece, width_q),
            k_gen.reshape(ranks, piece, width_kv),
            value_generator_rows.reshape(ranks, piece, width_kv),
            w_reward.reshape(heads, group, HEAD_WIDTH),
        )
    ])
    scored, reward = pl.pallas_call(
        functools.partial(to_generator_order, ranks, piece),
        out_shape=(pltpu.HBM((rows, width_q), bf16), pltpu.HBM((1, rows), f32)),
        in_specs=[smem, vmem, vmem],
        out_specs=(hbm, hbm),
        scratch_shapes=[pltpu.VMEM((1, rows), f32), dma((ranks + 1,))],
    )(order, pltpu.with_memory_space_constraint(hidden, pltpu.VMEM), pltpu.with_memory_space_constraint(reward, pltpu.VMEM))
    return (scored, reward.reshape(rows))


def solution(mesh):
    in_specs = (
        P(("groups", "dc", "sp"), "tp"),
        P(("groups", "dc", "sp"), "tp"),
        P(("groups", "dc", "sp"), "tp"),
        P("tp"),
        P(None, "groups"),
        P(("groups", "dc", "sp"), None),
    )
    out_specs = (P(("groups", "dc", "sp"), "tp"), P(("groups", "dc", "sp")))

    def whole(q_gen, k_gen, value_generator_rows, w_reward, plan, gen_order):
        rows = q_gen.shape[0] // (mesh.shape["groups"] * mesh.shape["dc"] * mesh.shape["sp"])
        heads = k_gen.shape[1] // HEAD_WIDTH // mesh.shape["tp"]
        fits = (
            mesh.shape["dc"] in (2, 4)
            and mesh.shape["sp"] == 2
            and heads % 2 == 0
            and rows == HEAD_WIDTH
            and rows % (16 * mesh.shape["dc"] * mesh.shape["sp"]) == 0
        )
        inner = gather_body if fits else body
        return jax.shard_map(inner, mesh=mesh, in_specs=in_specs, out_specs=out_specs, check_vma=False)(
            q_gen, k_gen, value_generator_rows, w_reward, plan, gen_order
        )

    return whole
```

```python
import functools

import jax
import jax.numpy as jnp
from jax import lax
from jax.experimental import pallas as pl
from jax.experimental.pallas import tpu as pltpu
from jax.sharding import PartitionSpec as P

HEAD_WIDTH = 128


NEG = -1e30


def from_behind(block, axis, distance):
    devices = range(lax.axis_size(axis))
    route = [(i - distance, i) for i in devices if i - distance in devices]
    return lax.ppermute(block, axis, route)


def fold_block(state, key_rows, value_rows, query_rows, allowed, scale):
    top, total, mixed = state
    scores = (
        jnp.einsum("rjge,nje->jgrn", query_rows, key_rows, preferred_element_type=jnp.float32)
        * scale
    )
    if allowed is not None:
        scores = jnp.where(allowed, scores, NEG)
    newtop = jnp.maximum(top, jnp.max(scores, axis=-1))
    shrink = jnp.exp(top - newtop)
    weight = jnp.exp(scores - newtop[..., None])
    if allowed is not None:
        weight = jnp.where(allowed, weight, 0.0)
    total = total * shrink + jnp.sum(weight, axis=-1)
    update = jnp.einsum(
        "jgrn,nje->jgre",
        weight.astype(jnp.bfloat16),
        value_rows,
        preferred_element_type=jnp.float32,
    )
    return (newtop, total, mixed * shrink[..., None] + update)


def body(q_gen, k_gen, value_generator_rows, w_reward, plan, gen_order):
    ranks = lax.axis_size(("dc", "sp"))
    sp_size = lax.axis_size("sp")
    dc_size = ranks // sp_size
    rows = q_gen.shape[0]
    piece = rows // ranks
    width_q = q_gen.shape[1]
    width_kv = k_gen.shape[1]
    heads_kv = width_kv // HEAD_WIDTH
    rollout_group = width_q // HEAD_WIDTH // heads_kv
    scale = HEAD_WIDTH ** (-0.5)
    order_row = gen_order[0]
    labels = jnp.arange(ranks, dtype=jnp.int32)
    inverse = jnp.sum(jnp.where(order_row[:, None] == labels[None, :], labels[:, None], 0), axis=0)
    q_send = jnp.take(q_gen.reshape(ranks, piece, width_q), inverse, axis=0)
    k_send = jnp.take(k_gen.reshape(ranks, piece, width_kv), inverse, axis=0)
    v_send = jnp.take(value_generator_rows.reshape(ranks, piece, width_kv), inverse, axis=0)
    q_flat = q_send.reshape(rows, width_q)
    k_flat = k_send.reshape(rows, width_kv)
    v_flat = v_send.reshape(rows, width_kv)
    query_layout, key_layout, value_layout = (
        lax.all_to_all(q_flat, ("dc", "sp"), split_axis=0, concat_axis=0, tiled=True),
        lax.all_to_all(k_flat, ("dc", "sp"), split_axis=0, concat_axis=0, tiled=True),
        lax.all_to_all(v_flat, ("dc", "sp"), split_axis=0, concat_axis=0, tiled=True),
    )
    me = lax.axis_index(("dc", "sp"))
    my_dc = me // sp_size
    start = plan[0, my_dc]
    length = plan[2, my_dc]
    local = jnp.arange(rows, dtype=jnp.int32)
    position = (my_dc - start) * (rows * sp_size) + me % sp_size * rows + local
    valid = position < length
    query_rows = query_layout.reshape(rows, heads_kv, rollout_group, HEAD_WIDTH)
    state = (
        jnp.full((heads_kv, rollout_group, rows), NEG, jnp.float32),
        jnp.zeros((heads_kv, rollout_group, rows), jnp.float32),
        jnp.zeros((heads_kv, rollout_group, rows, HEAD_WIDTH), jnp.float32),
    )
    causal = local[None, :] <= local[:, None]
    state = fold_block(
        state,
        key_layout.reshape(rows, heads_kv, HEAD_WIDTH),
        value_layout.reshape(rows, heads_kv, HEAD_WIDTH),
        query_rows,
        causal,
        scale,
    )
    own = jnp.stack([key_layout, value_layout])
    reach = max(dc_size // 2, 1) * sp_size

    def advance(step, carry):
        folded, moving = carry
        moving = from_behind(moving, ("dc", "sp"), 1)
        source = me - step - 1
        use = (source >= 0) & (source // sp_size >= start)
        folded = lax.cond(
            use,
            lambda carried: fold_block(
                carried,
                moving[0].reshape(rows, heads_kv, HEAD_WIDTH),
                moving[1].reshape(rows, heads_kv, HEAD_WIDTH),
                query_rows,
                None,
                scale,
            ),
            lambda carried: carried,
            folded,
        )
        return (folded, moving)

    state, _ = lax.fori_loop(0, reach - 1, advance, (state, own))
    top, total, mixed = state
    hidden = mixed / total[..., None]
    hidden = jnp.transpose(hidden, (2, 0, 1, 3)).reshape(rows, width_q)
    hidden = jnp.where(valid[:, None], hidden, 0.0).astype(jnp.bfloat16)
    back = lax.all_to_all(hidden, ("dc", "sp"), split_axis=0, concat_axis=0, tiled=True)
    scored = jnp.take(back.reshape(ranks, piece, width_q), order_row, axis=0).reshape(rows, width_q)
    partial_reward = jnp.sum(scored.astype(jnp.float32) * w_reward[None, :], axis=1)
    reward = lax.psum(partial_reward, "tp")
    return (scored, reward)


MESH = pl.DeviceIdType.MESH
BIG = -1e30


def gather_attend(
    sizes, order_hbm, plan_hbm, q_hbm, k_hbm, v_hbm, w_hbm, out_ref, rew_ref, order_out,
    order_ref, plan_ref, q_ref, k_ref, v_ref, w_ref, q_send, q_all, kv_send, kv_all, hid_send, racc, rew_all,
    kv_ssem, kv_rsem, fwd_ssem, q_ssem, q_rsem, hid_ssem, hid_rsem, rew_ssem, rew_rsem, in_sem,
):
    dcs, sps, tps, piece, rows, heads, group, jc, span, halves = sizes
    ranks, units, width = dcs * sps, jc * halves, group * HEAD_WIDTH
    dc, sp, tp = lax.axis_index("dc"), lax.axis_index("sp"), lax.axis_index("tp")
    me, other = dc * sps + sp, 1 - sp

    arguments = ((order_hbm, order_ref), (k_hbm, k_ref), (v_hbm, v_ref), (q_hbm, q_ref), (plan_hbm, plan_ref), (w_hbm, w_ref))
    loads = [pltpu.make_async_copy(a, b, in_sem.at[i]) for i, (a, b) in enumerate(arguments)]
    for load in loads[:3]:
        load.start()

    barrier = pltpu.get_barrier_semaphore()
    for rank in range(ranks):
        @pl.when(rank != me)
        def _():
            pl.semaphore_signal(
                barrier, inc=1, device_id={"dc": rank // sps, "sp": rank % sps}, device_id_type=MESH
            )
    for shift in range(1, tps):
        for core in range(sps):
            pl.semaphore_signal(
                barrier, inc=1, device_id={"tp": lax.rem(tp + shift, tps), "sp": core}, device_id_type=MESH
            )

    for load in loads[:3]:
        load.wait()
    for load in loads[3:]:
        load.start()
    segments = []
    for d in range(ranks):
        seg = jnp.int32(0)
        for s in range(1, ranks):
            seg = jnp.where(order_ref[0, s] == d, s, seg)
        segments.append(seg)
    def prepare(u):
        jj, h = u // halves, u % halves
        for dl in range(span):
            seg = segments[h * span + dl]
            for core in range(sps):
                cols = pl.ds((core * jc + jj) * HEAD_WIDTH, HEAD_WIDTH)
                kv_send[core, u, 0, pl.ds(dl * piece, piece), :] = k_ref[seg, :, cols]
                kv_send[core, u, 1, pl.ds(dl * piece, piece), :] = v_ref[seg, :, cols]

    prepare(0)
    pl.semaphore_wait(barrier, ranks - 1 + (tps - 1) * sps)

    steps = [sign * hop for hop in (1, 2) if hop < dcs for sign in (1, -1)]

    def direct(step):
        target = dc + step
        inside = (target >= 0) & (target < dcs)
        return inside if abs(step) == 1 else inside & (target > 0) & (target < dcs - 1)

    relays = ((1, (2, 3), 0), (2, (1, 0), 3)) if dcs == 4 else ()

    def cut(ref, *index, part):
        return ref.at[index if part is None else index + (part,)]

    def kv_copy(u, i, core, part):
        return pltpu.make_async_remote_copy(
            src_ref=cut(kv_send, core, u, part=part), dst_ref=cut(kv_all, u, me, part=part),
            send_sem=kv_ssem.at[u, part or 0, i * sps + core], recv_sem=kv_rsem.at[u, part or 0, me],
            device_id={"dc": dc + steps[i], "sp": core}, device_id_type=MESH,
        )

    def kv_copy_sibling(u, part):
        return pltpu.make_async_remote_copy(
            src_ref=cut(kv_send, other, u, part=part), dst_ref=cut(kv_all, u, me, part=part),
            send_sem=kv_ssem.at[u, part or 0, len(steps) * sps], recv_sem=kv_rsem.at[u, part or 0, me],
            device_id={"sp": other}, device_id_type=MESH,
        )

    def kv_forward(u, k, core, source_dc, target_dc, part):
        source = source_dc * sps + core
        return pltpu.make_async_remote_copy(
            src_ref=cut(kv_all, u, source, part=part), dst_ref=cut(kv_all, u, source, part=part),
            send_sem=fwd_ssem.at[u, part or 0, k * sps + core], recv_sem=kv_rsem.at[u, part or 0, source],
            device_id={"dc": target_dc}, device_id_type=MESH,
        )

    def kv_wait(u, source, part):
        pltpu.make_async_remote_copy(
            src_ref=cut(kv_all, u, source, part=part), dst_ref=cut(kv_all, u, source, part=part),
            send_sem=kv_ssem.at[u, part or 0, 0], recv_sem=kv_rsem.at[u, part or 0, source],
            device_id={"sp": other}, device_id_type=MESH,
        ).wait_recv()

    q_copy = pltpu.make_async_remote_copy(
        src_ref=q_send, dst_ref=q_all.at[1], send_sem=q_ssem, recv_sem=q_rsem,
        device_id={"sp": other}, device_id_type=MESH,
    )

    def send_unit(u, part):
        for i, step in enumerate(steps):
            @pl.when(direct(step))
            def _():
                for core in range(sps):
                    kv_copy(u, i, core, part).start()
        kv_copy_sibling(u, part).start()

    last = units - 1

    for u in range(last):
        send_unit(u, None)
        prepare(u + 1)
    for part in range(2):
        send_unit(last, part)
    for u in range(units):
        kv_all[u, me] = kv_send[sp, u]
    loads[3].wait()
    for d in range(ranks):
        h, dl = d // span, d % span
        for jj in range(jc):
            u = jj * halves + h
            mine = pl.ds(pl.multiple_of((sp * jc + jj) * width, width), width)
            theirs = pl.ds(pl.multiple_of((other * jc + jj) * width, width), width)
            q_send[u, dl] = q_ref[segments[d], :, theirs]
            q_all[0, u, dl] = q_ref[segments[d], :, mine]
    q_copy.start()
    for load in loads[4:]:
        load.wait()

    tile = 2 * group * piece
    row = lax.broadcasted_iota(jnp.int32, (tile, 1), 0)
    rank_of_row = dc * sps + jnp.where(row < group * piece, sp, other)
    offset = rank_of_row * piece + lax.rem(row, piece)
    column = lax.broadcasted_iota(jnp.int32, (tile, rows), 1)
    causal = jnp.where(column <= offset, 0.0, BIG)
    factor = HEAD_WIDTH ** (-0.5) * 1.4426950408889634

    def hid_place(u):
        head = sp * jc + u // halves
        return out_ref.at[
            pl.ds(lax.rem(u, halves) * span, span), :, pl.ds(pl.multiple_of(head * width, width), width)
        ]

    def hid_copy(u):
        return pltpu.make_async_remote_copy(
            src_ref=hid_send.at[u], dst_ref=hid_place(u),
            send_sem=hid_ssem.at[u], recv_sem=hid_rsem.at[u],
            device_id={"sp": other}, device_id_type=MESH,
        )

    def pass_on(u, part):
        for relay, fars, end in relays:
            @pl.when(dc == relay)
            def _():
                for k, far in enumerate(fars):
                    for core in range(sps):
                        kv_wait(u, far * sps + core, part)
                        kv_forward(u, k, core, far, end, part).start()

    def arrive(u, part):
        for source in range(ranks):
            waits = source != me
            for relay, fars, _ in relays:
                if source // sps in fars:
                    waits = waits & (dc != relay)

            @pl.when(waits)
            def _():
                kv_wait(u, source, part)

    def attend(u, split):
        jj, h = u // halves, lax.rem(u, halves)
        head = sp * jc + jj

        def plan_order(which):
            return jnp.concatenate(
                [
                    kv_all[u, source, which, pl.ds(dl * piece, piece), :]
                    for dl in range(span)
                    for source in range(ranks)
                ],
                axis=0,
            )

        arrive(u, 0 if split else None)
        keys = plan_order(0)
        weighed = []
        for dl in range(span):
            d = h * span + dl
            slot = d // sps
            n = (dl + 1) * rows
            query = jnp.concatenate(
                [
                    q_all[t, u, dl, :, pl.ds(g * HEAD_WIDTH, HEAD_WIDTH)]
                    for t in range(2)
                    for g in range(group)
                ],
                axis=0,
            )
            scores = lax.dot_general(
                query, keys[:n], (((1,), (1,)), ((), ())), preferred_element_type=jnp.float32
            )
            start = plan_ref[0, slot]
            blocks = []
            for d2 in range(dl + 1):
                block = scores[:, d2 * rows:(d2 + 1) * rows]
                if d2 == dl:
                    block = block + causal
                elif d2 // sps != dl // sps:
                    block = block + jnp.where(plan_ref[0, h * (span // sps) + d2 // sps] == start, 0.0, BIG)
                blocks.append(block)
            peak = blocks[0]
            for block in blocks[1:]:
                peak = jnp.maximum(peak, block)
            top = jnp.max(peak, axis=1, keepdims=True)
            weights = [jnp.exp2((block - top) * factor) for block in blocks]
            total = weights[0]
            for weight in weights[1:]:
                total = total + weight
            total = jnp.sum(total, axis=1, keepdims=True)
            weight16 = jnp.concatenate([weight.astype(jnp.bfloat16) for weight in weights], axis=1)
            base = (slot - start) * (rows * sps) + lax.rem(d, sps) * rows
            share = jnp.where(offset + base < plan_ref[2, slot], 1.0 / total, 0.0)
            weighed.append((weight16, share))
        if split:
            arrive(u, 1)
        values = plan_order(1)
        for dl, (weight16, share) in enumerate(weighed):
            d = h * span + dl
            mixed = jnp.dot(weight16, values[:(dl + 1) * rows], preferred_element_type=jnp.float32)
            hidden = (mixed * share).astype(jnp.bfloat16)
            for t in range(2):
                reward = jnp.zeros((piece, HEAD_WIDTH), jnp.float32)
                for g in range(group):
                    part = hidden[(t * group + g) * piece:(t * group + g + 1) * piece]
                    cols = pl.ds(g * HEAD_WIDTH, HEAD_WIDTH)
                    if t == 0:
                        out_ref[d, :, pl.ds(pl.multiple_of(head * width, width) + g * HEAD_WIDTH, HEAD_WIDTH)] = part
                    else:
                        hid_send[u, dl, :, cols] = part
                    w = w_ref[sp * jc + jj, pl.ds(g, 1), :]
                    reward = reward + part.astype(jnp.float32) * w
                racc[u, t, pl.ds(dl * piece, piece), :] = reward
        hid_copy(u).start()

    def attend_whole(u, carry):
        attend(u, False)
        return carry

    def pass_on_whole(u, carry):
        pass_on(u, None)
        return carry

    lax.fori_loop(0, last, pass_on_whole, 0)
    for part in range(2):
        pass_on(last, part)
    q_copy.wait_recv()
    lax.fori_loop(0, last, attend_whole, 0)
    attend(jnp.int32(last), True)

    slot_me = tp * sps + sp

    def rew_copy(shift, same):
        peer = lax.rem(tp + shift, tps)
        return pltpu.make_async_remote_copy(
            src_ref=rew_all.at[slot_me if same else tps * sps], dst_ref=rew_all.at[slot_me],
            send_sem=rew_ssem.at[2 * shift + (0 if same else 1)], recv_sem=rew_rsem.at[slot_me],
            device_id={"tp": peer, "sp": sp if same else other}, device_id_type=MESH,
        )

    pairs = [(shift, same) for shift in reversed(range(tps)) for same in (True, False) if (shift, same) != (0, True)]

    for t in range(2):
        cells = []
        for h in range(halves):
            cell = racc[h, t]
            for jj in range(1, jc):
                cell = cell + racc[jj * halves + h, t]
            cells.append(cell)
        line = jnp.sum(jnp.concatenate(cells, axis=0).T, axis=0, keepdims=True)
        rew_all[slot_me if t == 0 else tps * sps] = jnp.broadcast_to(line, (8, rows))
        for shift, same in pairs:
            if same == (t == 0):
                rew_copy(shift, same).start()

    for shift, same in pairs:
        rew_copy(shift, same).wait_send()
    q_copy.wait_send()

    def drain(u, part):
        kv_copy_sibling(u, part).wait_send()
        for i, step in enumerate(steps):
            @pl.when(direct(step))
            def _():
                for core in range(sps):
                    kv_copy(u, i, core, part).wait_send()
        for relay, fars, end in relays:
            @pl.when(dc == relay)
            def _():
                for k, far in enumerate(fars):
                    for core in range(sps):
                        kv_forward(u, k, core, far, end, part).wait_send()

    def drain_whole(u, carry):
        drain(u, None)
        return carry

    lax.fori_loop(0, last, drain_whole, 0)
    for part in range(2):
        drain(last, part)
    for u in range(units):
        hid_copy(u).wait()

    for source in range(tps * sps):
        @pl.when(source != slot_me)
        def _():
            pltpu.make_async_remote_copy(
                src_ref=rew_all.at[source], dst_ref=rew_all.at[source],
                send_sem=rew_ssem.at[0], recv_sem=rew_rsem.at[source],
                device_id={"sp": other}, device_id_type=MESH,
            ).wait_recv()
    reward = rew_all[0]
    for source in range(1, tps * sps):
        reward = reward + rew_all[source]
    rew_ref[...] = reward
    for s in range(ranks):
        order_out[0, s] = order_ref[0, s]


def to_generator_order(ranks, piece, order_ref, hidden, reward_ref, out, out_reward, line, sems):
    copies = [
        pltpu.make_async_copy(hidden.at[order_ref[0, s]], out.at[pl.ds(s * piece, piece)], sems.at[s])
        for s in range(ranks)
    ]
    for copy in copies:
        copy.start()
    reward = reward_ref[...]
    segment = lax.broadcasted_iota(jnp.int32, reward.shape, 1) // piece
    moved = reward
    for s in range(ranks):
        shift = lax.rem(s - order_ref[0, s] + ranks, ranks) * piece
        moved = jnp.where(segment == s, pltpu.roll(reward, shift, 1), moved)
    line[...] = moved[:1]
    last = pltpu.make_async_copy(line, out_reward, sems.at[ranks])
    last.start()
    for copy in copies + [last]:
        copy.wait()


def gather_body(q_gen, k_gen, value_generator_rows, w_reward, plan, gen_order):
    dcs, sps, tps = lax.axis_size("dc"), lax.axis_size("sp"), lax.axis_size("tp")
    ranks = dcs * sps
    rows, width_q = q_gen.shape
    width_kv = k_gen.shape[1]
    piece = rows // ranks
    heads = width_kv // HEAD_WIDTH
    group = width_q // width_kv
    jc = heads // sps
    span = max(dcs // 2, 1) * sps
    halves = ranks // span
    units, width = jc * halves, group * HEAD_WIDTH
    sizes = (dcs, sps, tps, piece, rows, heads, group, jc, span, halves)
    bf16, f32 = jnp.bfloat16, jnp.float32
    vmem, hbm = pl.BlockSpec(memory_space=pltpu.VMEM), pl.BlockSpec(memory_space=pltpu.HBM)
    smem = pl.BlockSpec(memory_space=pltpu.SMEM)
    dma = pltpu.SemaphoreType.DMA
    hidden, reward, order = pl.pallas_call(
        functools.partial(gather_attend, sizes),
        out_shape=(
            pltpu.VMEM((ranks, piece, width_q), bf16),
            pltpu.VMEM((8, rows), f32),
            pltpu.SMEM(gen_order.shape, jnp.int32),
        ),
        in_specs=[hbm] * 6,
        out_specs=(vmem, vmem, smem),
        scratch_shapes=[
            pltpu.SMEM(gen_order.shape, jnp.int32),
            pltpu.SMEM(plan.shape, jnp.int32),
            pltpu.VMEM((ranks, piece, width_q), bf16),
            pltpu.VMEM((ranks, piece, width_kv), bf16),
            pltpu.VMEM((ranks, piece, width_kv), bf16),
            pltpu.VMEM((heads, group, HEAD_WIDTH), f32),
            pltpu.VMEM((units, span, piece, width), bf16),
            pltpu.VMEM((2, units, span, piece, width), bf16),
            pltpu.VMEM((sps, units, 2, span * piece, HEAD_WIDTH), bf16),
            pltpu.VMEM((units, ranks, 2, span * piece, HEAD_WIDTH), bf16),
            pltpu.VMEM((units, span, piece, width), bf16),
            pltpu.VMEM((units, 2, span * piece, HEAD_WIDTH), f32),
            pltpu.VMEM((tps * sps + 1, 8, rows), f32),
            dma((units, 2, 4 * sps + 1)),
            dma((units, 2, ranks)),
            dma((units, 2, 2 * sps)),
            dma,
            dma,
            dma((units,)),
            dma((units,)),
            dma((2 * tps,)),
            dma((tps * sps,)),
            dma((6,)),
        ],
        compiler_params=pltpu.CompilerParams(
            collective_id=0, has_side_effects=True, vmem_limit_bytes=32 * 1024 * 1024
        ),
    )(*[
        pltpu.with_memory_space_constraint(operand, pltpu.HBM)
        for operand in (
            gen_order,
            plan,
            q_gen.reshape(ranks, piece, width_q),
            k_gen.reshape(ranks, piece, width_kv),
            value_generator_rows.reshape(ranks, piece, width_kv),
            w_reward.reshape(heads, group, HEAD_WIDTH),
        )
    ])
    scored, reward = pl.pallas_call(
        functools.partial(to_generator_order, ranks, piece),
        out_shape=(pltpu.HBM((rows, width_q), bf16), pltpu.HBM((1, rows), f32)),
        in_specs=[smem, vmem, vmem],
        out_specs=(hbm, hbm),
        scratch_shapes=[pltpu.VMEM((1, rows), f32), dma((ranks + 1,))],
    )(order, pltpu.with_memory_space_constraint(hidden, pltpu.VMEM), pltpu.with_memory_space_constraint(reward, pltpu.VMEM))
    return (scored, reward.reshape(rows))


def solution(mesh):
    in_specs = (
        P(("groups", "dc", "sp"), "tp"),
        P(("groups", "dc", "sp"), "tp"),
        P(("groups", "dc", "sp"), "tp"),
        P("tp"),
        P(None, "groups"),
        P(("groups", "dc", "sp"), None),
    )
    out_specs = (P(("groups", "dc", "sp"), "tp"), P(("groups", "dc", "sp")))

    def whole(q_gen, k_gen, value_generator_rows, w_reward, plan, gen_order):
        rows = q_gen.shape[0] // (mesh.shape["groups"] * mesh.shape["dc"] * mesh.shape["sp"])
        heads = k_gen.shape[1] // HEAD_WIDTH // mesh.shape["tp"]
        fits = (
            mesh.shape["dc"] in (2, 4)
            and mesh.shape["sp"] == 2
            and heads % 2 == 0
            and rows == HEAD_WIDTH
            and rows % (16 * mesh.shape["dc"] * mesh.shape["sp"]) == 0
        )
        inner = gather_body if fits else body
        return jax.shard_map(inner, mesh=mesh, in_specs=in_specs, out_specs=out_specs, check_vma=False)(
            q_gen, k_gen, value_generator_rows, w_reward, plan, gen_order
        )

    return whole
```
